512 devices in a mesh: tower: 2 (over z_hi), ctx: 128 (over z_lo, x, y), dp: 2 (over core).
Axes of the slice: x: 4, y: 4, z: 16 (z_hi: 2, z_lo: 8; z = z_hi * 8 + z_lo), core: 2. Of those that a mesh axis runs over, the one named last changes fastest.
Arguments:
- query_self: bfloat16 [2, 32768, 512], P('tower', ('dp', 'ctx')), parts along dimension 1, may hold values from -6 to 6
- key_self: bfloat16 [2, 32768, 512], P('tower', ('dp', 'ctx')), parts along dimension 1, may hold values from -6 to 6
- value_self: bfloat16 [2, 32768, 512], P('tower', ('dp', 'ctx')), parts along dimension 1, may hold values from -6 to 6
- query_cross: bfloat16 [2, 32768, 512], P('tower', ('dp', 'ctx')), parts along dimension 1, may hold values from -6 to 6
- key_cross: bfloat16 [2, 32768, 512], P('tower', ('dp', 'ctx')), parts along dimension 1, may hold values from -6 to 6
- value_cross: bfloat16 [2, 32768, 512], P('tower', ('dp', 'ctx')), parts along dimension 1, may hold values from -6 to 6
- cotangent: bfloat16 [2, 32768, 512], P('tower', ('dp', 'ctx')), parts along dimension 1, may hold values from -6 to 6
- block_slot: int32 [128], P('ctx'), may hold values from 0 to 127, as said below
Outputs:
- attended: bfloat16 [2, 32768, 512], P('tower', ('dp', 'ctx')), parts along dimension 1
- query_grad_self: bfloat16 [2, 32768, 512], P('tower', ('dp', 'ctx')), parts along dimension 1
- key_grad_self: bfloat16 [2, 32768, 512], P('tower', ('dp', 'ctx')), parts along dimension 1
- value_grad_self: bfloat16 [2, 32768, 512], P('tower', ('dp', 'ctx')), parts along dimension 1
- query_grad_cross: bfloat16 [2, 32768, 512], P('tower', ('dp', 'ctx')), parts along dimension 1
- key_grad_cross: bfloat16 [2, 32768, 512], P('tower', ('dp', 'ctx')), parts along dimension 1
- value_grad_cross: bfloat16 [2, 32768, 512], P('tower', ('dp', 'ctx')), parts along dimension 1
The draws below stay inside these ranges and needn't reach their ends.
There are 2 independent parts, one for each index of `dp`. The reference program is written for one: setup_inputs(seed, part) draws one part's arguments, and reference() takes and returns one part's arrays. A program takes and returns all parts, laid end to end along the dimension named above; an argument that names none is the same for every part. Nothing has to cross between parts.
Inputs may be any that keep to these rules, and one draw needn't show every extreme that they name: `block_slot`: there is one offset c such that entry b is (b + c) modulo 128.
All inputs are finite; a program needn't handle non-finite values.
Results may differ from the reference program's by a relative error of at most 0.04.
Values may be sent and summed in bfloat16 or wider, within the bound.
No kernel may reach another device: no remote copies, remote signals or barrier semaphores. Data moves between devices by JAX's collectives and lax.ppermute only.
A program may use at most 64 MiB of HBM per device.

```python
import jax
import jax.numpy as jnp
from jax import lax

HEADS = 8
HEAD = 64
ROWS = 128
GROUP = 8
BLOCKS = 128
TOKENS = 16384


def aligned_pair(key, salt):
    key = jax.random.fold_in(key, salt)
    first, second = jax.random.split(key, 2)
    feature_count = HEADS * HEAD
    shape = (2, TOKENS, feature_count)
    query = jnp.clip(jax.random.normal(first, shape, jnp.float32), -6.0, 6.0)
    keys = jnp.clip(jax.random.normal(second, shape, jnp.float32), -6.0, 6.0)
    inside = jnp.arange(TOKENS) % ROWS
    picked = (inside % 16 == 5)[None, :, None]
    before = (inside % 16 == 4)[None, :, None]
    query = jnp.where(picked, query, query)
    keys = jnp.where(picked, keys, keys)
    keys = jnp.where(before, keys, keys)
    return (query.astype(jnp.bfloat16), keys.astype(jnp.bfloat16))


def draw_query_self(key, part):
    return aligned_pair(key, 3)[0]


def draw_key_self(key, part):
    return aligned_pair(key, 3)[1]


def draw_query_cross(key, part):
    return aligned_pair(key, 4)[0]


def draw_key_cross(key, part):
    return aligned_pair(key, 4)[1]


def draw_block_slot(key, part):
    key = jax.random.fold_in(key, 9)
    offset = jax.random.randint(key, (), 0, BLOCKS)
    return ((jnp.arange(BLOCKS, dtype=jnp.int32) + offset) % BLOCKS).astype(jnp.int32)


def levels(key, extent, cuts, least, high):
    def one(axis_at, shards_of):
        steps = jax.random.uniform(jax.random.fold_in(jax.random.fold_in(key, 6), axis_at), (shards_of,), jnp.float32, least / len(cuts), high / len(cuts))
        return jnp.repeat(jnp.exp(steps), extent[axis_at] // shards_of).reshape((-1,) + (1,) * (len(extent) - axis_at - 1))

    gain = one(*cuts[0])
    for cut in cuts[1:]:
        gain = gain * one(*cut)
    return gain


def centred(rng, shape, spread, bound, cuts=(), kind=jnp.bfloat16):
    values = spread * jax.random.normal(rng, shape, jnp.float32)
    if cuts:
        values = values * levels(rng, shape, cuts, -0.22, 0.18)
    return jnp.clip(values, -bound, bound).astype(kind)


def setup_inputs(seed: int = 0, part: int = 0) -> dict:
    key_list = jax.random.split(jax.random.key(seed), 9)
    part_splits = jax.random.split(jax.random.fold_in(key_list[8], part), 9)
    query_self = draw_query_self(jax.random.fold_in(jax.random.fold_in(key_list[8], part), 71), part)
    key_self = draw_key_self(jax.random.fold_in(jax.random.fold_in(key_list[8], part), 71), part)
    value_self = centred(part_splits[2], (2, TOKENS, HEADS * HEAD), 1.0, 6.0, ((0, 2), (1, 128)))
    query_cross = draw_query_cross(jax.random.fold_in(jax.random.fold_in(key_list[8], part), 71), part)
    key_cross = draw_key_cross(jax.random.fold_in(jax.random.fold_in(key_list[8], part), 71), part)
    value_cross = centred(part_splits[5], (2, TOKENS, HEADS * HEAD), 1.0, 6.0, ((0, 2), (1, 128)))
    cotangent = centred(part_splits[6], (2, TOKENS, HEADS * HEAD), 1.0, 6.0, ((0, 2), (1, 128)))
    block_slot = draw_block_slot(jax.random.fold_in(key_list[8], 71), part)
    return dict(query_self=query_self, key_self=key_self, value_self=value_self, query_cross=query_cross, key_cross=key_cross, value_cross=value_cross, cotangent=cotangent, block_slot=block_slot)


def rounded(matrix):
    return lax.optimization_barrier(matrix.astype(jnp.bfloat16)).astype(jnp.float32)


def attend(query, keys, values, upstream, block):
    query_count = query.shape[0]
    key_count = keys.shape[0]
    score_scale = HEAD ** -0.5
    query_heads = query.astype(jnp.float32).reshape(query_count, HEADS, HEAD)
    key_heads = keys.astype(jnp.float32).reshape(key_count, HEADS, HEAD)
    value_heads = values.astype(jnp.float32).reshape(key_count, HEADS, HEAD)
    upstream_heads = upstream.astype(jnp.float32).reshape(query_count, HEADS, HEAD)
    query_position = block * ROWS + jnp.arange(query_count, dtype=jnp.int32)
    key_position = (block - GROUP + 1) * ROWS + jnp.arange(key_count, dtype=jnp.int32)
    visible = (key_position[None, :] <= query_position[:, None]) & (key_position[None, :] >= 0)
    scores = jnp.einsum("ihd,jhd->hij", query_heads, key_heads) * score_scale
    scores = jnp.where(visible[None], scores, -1e30)
    row_max = jnp.max(scores, axis=2)
    log_total = row_max + jnp.log(jnp.sum(jnp.exp(scores - row_max[:, :, None]), axis=2))
    probabilities = jnp.where(visible[None], jnp.exp(scores - log_total[:, :, None]), 0.0)
    weights = rounded(probabilities)
    output = jnp.einsum("hij,jhd->ihd", weights, value_heads)
    delta = jnp.sum(upstream_heads * output, axis=2).T
    grad_value = jnp.einsum("hij,ihd->jhd", weights, upstream_heads)
    grad_probs = jnp.einsum("ihd,jhd->hij", upstream_heads, value_heads)
    grad_scores = rounded(probabilities * (grad_probs - delta[:, :, None]))
    grad_query = jnp.einsum("hij,jhd->ihd", grad_scores, key_heads) * score_scale
    grad_key = jnp.einsum("hij,ihd->jhd", grad_scores, query_heads) * score_scale
    feature_count = HEADS * HEAD
    return (output.reshape(query_count, feature_count), grad_query.reshape(query_count, feature_count),
            grad_key.reshape(key_count, feature_count), grad_value.reshape(key_count, feature_count))


def add_window(total, piece, start):
    window = lax.dynamic_slice_in_dim(total, start, piece.shape[0], 0)
    return lax.dynamic_update_slice_in_dim(total, window + piece, start, 0)


def reference(query_self, key_self, value_self, query_cross, key_cross, value_cross, cotangent, block_slot):
    feature_count = HEADS * HEAD
    order = jnp.argsort(block_slot).astype(jnp.int32)
    slots = block_slot.astype(jnp.int32)
    margin = (GROUP - 1) * ROWS

    def to_sequence(matrix):
        return matrix.reshape(BLOCKS, ROWS, feature_count)[order].reshape(BLOCKS * ROWS, feature_count)

    def from_sequence(matrix):
        return matrix.reshape(BLOCKS, ROWS, feature_count)[slots].reshape(BLOCKS * ROWS, feature_count)

    def padded(matrix):
        return jnp.concatenate([jnp.zeros((margin, feature_count), matrix.dtype), matrix], axis=0)

    attended_list = [None, None]
    self_grads = [[None, None], [None, None], [None, None]]
    cross_grads = [[None, None], [None, None], [None, None]]
    for tower in range(2):
        partner = 1 - tower
        query_s = to_sequence(query_self[tower])
        query_c = to_sequence(query_cross[tower])
        upstream = to_sequence(cotangent[tower])
        key_s = padded(to_sequence(key_self[tower]))
        value_s = padded(to_sequence(value_self[tower]))
        key_c = padded(to_sequence(key_cross[partner]))
        value_c = padded(to_sequence(value_cross[partner]))

        def step(carry, block):
            grad_ks, grad_vs, grad_kc, grad_vc = carry
            row_start = block * ROWS
            rows_q_s = lax.dynamic_slice_in_dim(query_s, row_start, ROWS, 0)
            rows_q_c = lax.dynamic_slice_in_dim(query_c, row_start, ROWS, 0)
            rows_up = lax.dynamic_slice_in_dim(upstream, row_start, ROWS, 0)
            first = attend(rows_q_s, lax.dynamic_slice_in_dim(key_s, row_start, GROUP * ROWS, 0),
                           lax.dynamic_slice_in_dim(value_s, row_start, GROUP * ROWS, 0), rows_up, block)
            second = attend(rows_q_c, lax.dynamic_slice_in_dim(key_c, row_start, GROUP * ROWS, 0),
                            lax.dynamic_slice_in_dim(value_c, row_start, GROUP * ROWS, 0), rows_up, block)
            carry = (add_window(grad_ks, first[2], row_start), add_window(grad_vs, first[3], row_start),
                     add_window(grad_kc, second[2], row_start), add_window(grad_vc, second[3], row_start))
            return carry, (first[0] + second[0], first[1], second[1])

        zero_grad = jnp.zeros((margin + BLOCKS * ROWS, feature_count), jnp.float32)
        carry, outputs = lax.scan(step, (zero_grad, zero_grad, zero_grad, zero_grad), jnp.arange(BLOCKS, dtype=jnp.int32))
        combined, qgrad_s, qgrad_c = [from_sequence(item.reshape(BLOCKS * ROWS, feature_count)) for item in outputs]
        grad_ks, grad_vs, grad_kc, grad_vc = [from_sequence(item[margin:]) for item in carry]
        attended_list[tower] = combined.astype(jnp.bfloat16)
        self_grads[0][tower] = qgrad_s.astype(jnp.bfloat16)
        self_grads[1][tower] = grad_ks.astype(jnp.bfloat16)
        self_grads[2][tower] = grad_vs.astype(jnp.bfloat16)
        cross_grads[0][tower] = qgrad_c.astype(jnp.bfloat16)
        cross_grads[1][partner] = grad_kc.astype(jnp.bfloat16)
        cross_grads[2][partner] = grad_vc.astype(jnp.bfloat16)
    return (jnp.stack(attended_list), jnp.stack(self_grads[0]), jnp.stack(self_grads[1]), jnp.stack(self_grads[2]),
            jnp.stack(cross_grads[0]), jnp.stack(cross_grads[1]), jnp.stack(cross_grads[2]))
```

```python
import jax
import jax.numpy as jnp
from jax import lax
from jax.experimental import pallas as pl
from jax.experimental.pallas import tpu as pltpu
from jax.sharding import PartitionSpec as P

HEADS = 8
HEAD = 64
ROWS = 128
GROUP = 8
TEAM = 8
PAIR = 2 * HEAD
BOTH = 2 * ROWS
HALO = GROUP - 1
WINDOW = GROUP * ROWS
SPAN = (HALO + TEAM) * ROWS
FEATURES = HEADS * HEAD
VMEM_BYTES = 48 * 1024 * 1024
SELF, CROSS, NEAR, FAR = 0, 1, 2, 3


def vmem(count):
    return [pl.BlockSpec(memory_space=pltpu.VMEM)] * count


def smem():
    return [pl.BlockSpec(memory_space=pltpu.SMEM)]


def block_shape(*lead, dtype=jnp.bfloat16):
    return jax.ShapeDtypeStruct((*lead, ROWS, PAIR), dtype)


def paired(left, right, h):
    lanes = pl.ds(h * HEAD, HEAD)
    return jnp.concatenate([left[:, lanes], right[:, lanes]], axis=1)


def my_flip():
    return lax.rem(lax.axis_index("ctx") // TEAM, 2) * (TEAM // 2)


def pack_kernel(
    query_s, key_s, value_s, query_c, key_c, value_c, upstream, out, held, arrived
):
    sources = (upstream, query_c, query_s, key_s, value_s, key_c, value_c)
    copies = [
        pltpu.make_async_copy(source, held.at[i], arrived.at[i])
        for i, source in enumerate(sources)
    ]
    for copy in copies:
        copy.start()
    flip = my_flip()
    copies[0].wait()
    for kind, left, right in ((FAR, 1, 0), (NEAR, 2, 0), (SELF, 3, 4), (CROSS, 5, 6)):
        copies[left].wait()
        if right:
            copies[right].wait()
        for h in range(HEADS):
            out[jnp.bitwise_xor(h, flip), kind] = paired(held.at[left], held.at[right], h)


def attention_kernel(kind, slots, *refs):
    if kind == SELF:
        own, halo, out, dkv_own, dkv_halo, kv_t, scores, probs, stacks = refs
        queries = [own.at[b, NEAR] for b in range(TEAM)]
    else:
        qdo, own, halo, out, dkv_own, dkv_halo, kv_t, scores, probs, stacks = refs
        queries = [qdo.at[b] for b in range(TEAM)]
    blocks = [halo.at[b, kind] for b in range(HALO)] + [own.at[b, kind] for b in range(TEAM)]
    first_half = lax.broadcasted_iota(jnp.int32, (ROWS, PAIR), 1) < HEAD
    causal = lax.broadcasted_iota(jnp.int32, (ROWS, ROWS), 0) <= lax.broadcasted_iota(
        jnp.int32, (ROWS, ROWS), 1
    )
    peaks, hidden, sums = {}, {}, {}

    def turn(w):
        kv_t[:, w * ROWS : (w + 1) * ROWS] = blocks[w][...].T

    def begin(m):
        both = queries[m][...]
        none = jnp.zeros_like(both)
        stacks[m * BOTH : m * BOTH + ROWS, :] = jnp.where(
            first_half, both * jnp.bfloat16(HEAD ** (-0.5)), none
        )
        stacks[m * BOTH + ROWS : (m + 1) * BOTH, :] = jnp.where(first_half, none, both)
        slot = lax.rem(slots[0] + m, slots[1])
        hidden[m] = [jnp.where(slot >= HALO - k, 0.0, 1e30) for k in range(HALO)] + [0.0]

    def score(m, k):
        part = lax.dot_general(
            blocks[m + k][...],
            stacks[m * BOTH : (m + 1) * BOTH, :],
            (((1,), (1,)), ((), ())),
            preferred_element_type=jnp.float32,
        )
        logits = part[:, :ROWS]
        if k == GROUP - 1:
            logits = jnp.where(causal, logits, -1e30)
        scores[m % 2, k, :, :ROWS] = logits
        scores[m % 2, k, :, ROWS:] = part[:, ROWS:]
        peak = jnp.max(logits.reshape(ROWS // 8, 8, ROWS), axis=0) - hidden[m][k]
        peaks[m] = peak if k == 0 else jnp.maximum(peaks[m], peak)

    def raise_up(m, k, top):
        raised = jnp.exp(scores[m % 2, k, :, :ROWS] - (top + hidden[m][k]))
        change = raised * scores[m % 2, k, :, ROWS:]
        scores[m % 2, k, :, :ROWS] = raised
        total = jnp.sum(raised.reshape(ROWS // 8, 8, ROWS), axis=0)
        weighted = jnp.sum(change.reshape(ROWS // 8, 8, ROWS), axis=0)
        sums[m] = (total, weighted) if k == 0 else (sums[m][0] + total, sums[m][1] + weighted)

    def settle(m, k, scale, delta):
        weight = scores[m % 2, k, :, :ROWS] * scale
        change = weight * (scores[m % 2, k, :, ROWS:] - delta)
        rows, lanes = slice((m + k) * ROWS, (m + k + 1) * ROWS), m * BOTH
        probs[rows, lanes : lanes + ROWS] = change.astype(jnp.bfloat16)
        probs[rows, lanes + ROWS : lanes + BOTH] = weight.astype(jnp.bfloat16)

    def query_side(m):
        window, lanes = slice(m * ROWS, m * ROWS + WINDOW), m * BOTH
        mixed = lax.dot_general(
            kv_t[:, window],
            probs[window, lanes : lanes + BOTH],
            (((1,), (0,)), ((), ())),
            preferred_element_type=jnp.float32,
        )
        result = jnp.concatenate(
            [mixed[:HEAD, :ROWS] * HEAD ** (-0.5), mixed[HEAD:, ROWS:]], axis=0
        )
        out[m] = result.T.astype(jnp.bfloat16)

    def key_side(w):
        low, high = max(0, w - HALO), min(TEAM - 1, w) + 1
        total = lax.dot_general(
            probs[w * ROWS : (w + 1) * ROWS, low * BOTH : high * BOTH],
            stacks[low * BOTH : high * BOTH, :],
            (((1,), (0,)), ((), ())),
            preferred_element_type=jnp.float32,
        )
        if w < HALO:
            dkv_halo[w] = total.astype(jnp.bfloat16)
        else:
            dkv_own[w - HALO] = total

    begin(0)
    for k in range(GROUP):
        score(0, k)
        turn(k)
    for m in range(TEAM):
        top = jnp.max(peaks[m], axis=0, keepdims=True)
        if m + 1 < TEAM:
            begin(m + 1)
        for k in range(GROUP):
            raise_up(m, k, top)
            if m + 1 < TEAM:
                score(m + 1, k)
        if m + 1 < TEAM:
            turn(m + GROUP)
        scale = 1.0 / jnp.sum(sums[m][0], axis=0, keepdims=True)
        delta = jnp.sum(sums[m][1], axis=0, keepdims=True) * scale
        for k in range(GROUP):
            settle(m, k, scale, delta)
            if m and k == 1:
                query_side(m - 1)
            if m and k == 4:
                key_side(m - 1)
    query_side(TEAM - 1)
    for w in range(TEAM - 1, HALO + TEAM):
        key_side(w)


def attention(kind, *operands):
    def kernel(*refs):
        attention_kernel(kind, *refs)

    return pl.pallas_call(
        kernel,
        out_shape=(
            block_shape(TEAM),
            block_shape(TEAM, dtype=jnp.float32),
            block_shape(HALO),
        ),
        in_specs=smem() + vmem(len(operands) - 1),
        out_specs=tuple(vmem(3)),
        scratch_shapes=[
            pltpu.VMEM((PAIR, SPAN), jnp.bfloat16),
            pltpu.VMEM((2, GROUP, ROWS, BOTH), jnp.float32),
            pltpu.VMEM((SPAN, TEAM * BOTH), jnp.bfloat16),
            pltpu.VMEM((TEAM * BOTH, PAIR), jnp.bfloat16),
        ],
        compiler_params=pltpu.CompilerParams(vmem_limit_bytes=VMEM_BYTES),
        cost_estimate=pl.CostEstimate(flops=0, bytes_accessed=0, transcendentals=0),
        name="attention_cross" if kind == CROSS else "attention_self",
    )(*operands)


def join_kernel(own_s, own_c, home_s, home_c, out_s, out_c, out):
    for kind, own, home in ((SELF, own_s, home_s), (CROSS, own_c, home_c)):
        out[0, kind] = own[0].astype(jnp.bfloat16)
        for b in range(HALO):
            out[b + 1, kind] = (own[b + 1] + home[b].astype(jnp.float32)).astype(jnp.bfloat16)
    for b in range(TEAM):
        out[b, NEAR] = out_s[b]
        out[b, FAR] = out_c[b]


def halves(first, second):
    left = jnp.concatenate([first[:, :HEAD], second[:, :HEAD]], axis=1)
    right = jnp.concatenate([first[:, HEAD:], second[:, HEAD:]], axis=1)
    return left, right


def unpack_kernel(parts, attended, query_s, key_s, value_s, query_c, key_c, value_c):
    flip = my_flip()
    for h in range(0, HEADS, 2):
        lanes = pl.ds(h * HEAD, PAIR)
        first, second = parts.at[jnp.bitwise_xor(h, flip)], parts.at[jnp.bitwise_xor(h + 1, flip)]
        key_s[:, lanes], value_s[:, lanes] = halves(first[SELF], second[SELF])
        key_c[:, lanes], value_c[:, lanes] = halves(first[CROSS], second[CROSS])
        query_s[:, lanes], near = halves(first[NEAR], second[NEAR])
        query_c[:, lanes], far = halves(first[FAR], second[FAR])
        total = near.astype(jnp.float32) + far.astype(jnp.float32)
        attended[:, lanes] = total.astype(jnp.bfloat16)


def local_call(kernel, out_shape, in_specs, operands, name, scratch=()):
    return pl.pallas_call(
        kernel,
        out_shape=out_shape,
        in_specs=in_specs,
        out_specs=jax.tree.map(lambda shape: vmem(1)[0], out_shape),
        scratch_shapes=scratch,
        compiler_params=pltpu.CompilerParams(vmem_limit_bytes=VMEM_BYTES),
        cost_estimate=pl.CostEstimate(flops=0, bytes_accessed=0, transcendentals=0),
        name=name,
    )(*operands)


def to_next_team(value, step):
    count = lax.axis_size("ctx")
    route = [(i, (i + step * TEAM) % count ^ (TEAM // 2)) for i in range(count)]
    return lax.ppermute(value, "ctx", route)


def within_team(value):
    count = lax.axis_size("ctx")
    teams = [list(range(at, at + TEAM)) for at in range(0, count, TEAM)]
    return lax.all_to_all(value, "ctx", 0, 0, axis_index_groups=teams, tiled=True)


def swapped(value):
    return lax.ppermute(value, "tower", [(0, 1), (1, 0)])


def body(
    query_self, key_self, value_self, query_cross, key_cross, value_cross, cotangent, block_slot
):
    count = lax.axis_size("ctx")
    member = lax.rem(lax.axis_index("ctx"), TEAM)
    slots = jnp.stack([lax.rem(block_slot[0] - member + count, count), jnp.int32(count)])
    flat = jax.ShapeDtypeStruct((ROWS, FEATURES), jnp.bfloat16)
    inputs = (query_self, key_self, value_self, query_cross, key_cross, value_cross, cotangent)
    packed = local_call(
        pack_kernel,
        block_shape(TEAM, 4),
        [pl.BlockSpec(memory_space=pltpu.HBM)] * 7,
        tuple(pltpu.with_memory_space_constraint(value[0], pltpu.HBM) for value in inputs),
        "pack",
        [pltpu.VMEM((7, ROWS, FEATURES), jnp.bfloat16), pltpu.SemaphoreType.DMA((7,))],
    )
    own = within_team(packed)
    halo = to_next_team(own[1:, :NEAR], 1)
    crossing = swapped(own[:, FAR])
    out_s, own_s, back_s = attention(SELF, slots, own, halo)
    crossing, own_s = lax.optimization_barrier((crossing, own_s))
    out_c, own_c, back_c = attention(CROSS, slots, crossing, own, halo)
    home_s = to_next_team(back_s, -1)
    home_c = to_next_team(back_c, -1)
    joined = local_call(
        join_kernel,
        block_shape(TEAM, 4),
        vmem(6),
        (own_s, own_c, home_s, home_c, out_s, swapped(out_c)),
        "join",
    )
    outs = local_call(unpack_kernel, (flat,) * 7, vmem(1), (within_team(joined),), "unpack")
    return tuple(part[None] for part in outs)


def solution(mesh):
    rows = P("tower", ("dp", "ctx"), None)
    return jax.shard_map(
        body,
        mesh=mesh,
        in_specs=(rows,) * 7 + (P("ctx"),),
        out_specs=(rows,) * 7,
        check_vma=False,
    )
```

```python
import jax
import jax.numpy as jnp
from jax import lax
from jax.experimental import pallas as pl
from jax.experimental.pallas import tpu as pltpu
from jax.sharding import PartitionSpec as P

HEADS = 8
HEAD = 64
ROWS = 128
GROUP = 8
TEAM = 8
PAIR = 2 * HEAD
BOTH = 2 * ROWS
HALO = GROUP - 1
WINDOW = GROUP * ROWS
SPAN = (HALO + TEAM) * ROWS
FEATURES = HEADS * HEAD
VMEM_BYTES = 48 * 1024 * 1024
SELF, CROSS, NEAR, FAR = 0, 1, 2, 3


def vmem(count):
    return [pl.BlockSpec(memory_space=pltpu.VMEM)] * count


def smem():
    return [pl.BlockSpec(memory_space=pltpu.SMEM)]


def block_shape(*lead, dtype=jnp.bfloat16):
    return jax.ShapeDtypeStruct((*lead, ROWS, PAIR), dtype)


def paired(left, right, h):
    lanes = pl.ds(h * HEAD, HEAD)
    return jnp.concatenate([left[:, lanes], right[:, lanes]], axis=1)


def my_flip():
    return lax.rem(lax.axis_index("ctx") // TEAM, 2) * (TEAM // 2)


def pack_kernel(
    query_s, key_s, value_s, query_c, key_c, value_c, upstream, far, near, held, arrived
):
    sources = (upstream, query_c, query_s, key_s, value_s, key_c, value_c)
    copies = [
        pltpu.make_async_copy(source, held.at[i], arrived.at[i])
        for i, source in enumerate(sources)
    ]
    for copy in copies:
        copy.start()
    flip = my_flip()
    copies[0].wait()
    for kind, left, right in ((FAR, 1, 0), (NEAR, 2, 0), (SELF, 3, 4), (CROSS, 5, 6)):
        copies[left].wait()
        if right:
            copies[right].wait()
        for h in range(HEADS):
            value = paired(held.at[left], held.at[right], h)
            if kind == FAR:
                far[jnp.bitwise_xor(h, flip)] = value
            else:
                near[jnp.bitwise_xor(h, flip), kind] = value


def attention_kernel(kind, slots, *refs):
    if kind == SELF:
        own, halo, out, dkv_own, dkv_halo, kv_t, scores, probs, stacks = refs
        queries = [own.at[b, NEAR] for b in range(TEAM)]
    else:
        qdo, own, halo, out, dkv_own, dkv_halo, kv_t, scores, probs, stacks = refs
        queries = [qdo.at[b] for b in range(TEAM)]
    blocks = [halo.at[b, kind] for b in range(HALO)] + [own.at[b, kind] for b in range(TEAM)]
    first_half = lax.broadcasted_iota(jnp.int32, (ROWS, PAIR), 1) < HEAD
    causal = lax.broadcasted_iota(jnp.int32, (ROWS, ROWS), 0) <= lax.broadcasted_iota(
        jnp.int32, (ROWS, ROWS), 1
    )
    peaks, hidden, sums = {}, {}, {}

    def turn(w):
        kv_t[:, w * ROWS : (w + 1) * ROWS] = blocks[w][...].T

    def begin(m):
        both = queries[m][...]
        none = jnp.zeros_like(both)
        stacks[m * BOTH : m * BOTH + ROWS, :] = jnp.where(
            first_half, both * jnp.bfloat16(HEAD ** (-0.5)), none
        )
        stacks[m * BOTH + ROWS : (m + 1) * BOTH, :] = jnp.where(first_half, none, both)
        slot = lax.rem(slots[0] + m, slots[1])
        hidden[m] = [jnp.where(slot >= HALO - k, 0.0, 1e30) for k in range(HALO)] + [0.0]

    def score(m, k):
        part = lax.dot_general(
            blocks[m + k][...],
            stacks[m * BOTH : (m + 1) * BOTH, :],
            (((1,), (1,)), ((), ())),
            preferred_element_type=jnp.float32,
        )
        logits = part[:, :ROWS]
        if k == GROUP - 1:
            logits = jnp.where(causal, logits, -1e30)
        scores[m % 2, k, :, :ROWS] = logits
        scores[m % 2, k, :, ROWS:] = part[:, ROWS:]
        peak = jnp.max(logits.reshape(ROWS // 8, 8, ROWS), axis=0) - hidden[m][k]
        peaks[m] = peak if k == 0 else jnp.maximum(peaks[m], peak)

    def raise_up(m, k, top):
        raised = jnp.exp(scores[m % 2, k, :, :ROWS] - (top + hidden[m][k]))
        change = raised * scores[m % 2, k, :, ROWS:]
        scores[m % 2, k, :, :ROWS] = raised
        total = jnp.sum(raised.reshape(ROWS // 8, 8, ROWS), axis=0)
        weighted = jnp.sum(change.reshape(ROWS // 8, 8, ROWS), axis=0)
        sums[m] = (total, weighted) if k == 0 else (sums[m][0] + total, sums[m][1] + weighted)

    def settle(m, k, scale, delta):
        weight = scores[m % 2, k, :, :ROWS] * scale
        change = weight * (scores[m % 2, k, :, ROWS:] - delta)
        rows, lanes = slice((m + k) * ROWS, (m + k + 1) * ROWS), m * BOTH
        probs[rows, lanes : lanes + ROWS] = change.astype(jnp.bfloat16)
        probs[rows, lanes + ROWS : lanes + BOTH] = weight.astype(jnp.bfloat16)

    def query_side(m):
        window, lanes = slice(m * ROWS, m * ROWS + WINDOW), m * BOTH
        mixed = lax.dot_general(
            kv_t[:, window],
            probs[window, lanes : lanes + BOTH],
            (((1,), (0,)), ((), ())),
            preferred_element_type=jnp.float32,
        )
        result = jnp.concatenate(
            [mixed[:HEAD, :ROWS] * HEAD ** (-0.5), mixed[HEAD:, ROWS:]], axis=0
        )
        out[m] = result.T.astype(jnp.bfloat16)

    def key_side(w):
        low, high = max(0, w - HALO), min(TEAM - 1, w) + 1
        total = lax.dot_general(
            probs[w * ROWS : (w + 1) * ROWS, low * BOTH : high * BOTH],
            stacks[low * BOTH : high * BOTH, :],
            (((1,), (0,)), ((), ())),
            preferred_element_type=jnp.float32,
        )
        if w < HALO:
            dkv_halo[w] = total.astype(jnp.bfloat16)
        else:
            dkv_own[w - HALO] = total

    begin(0)
    for k in range(GROUP):
        score(0, k)
        turn(k)
    for m in range(TEAM):
        top = jnp.max(peaks[m], axis=0, keepdims=True)
        if m + 1 < TEAM:
            begin(m + 1)
        for k in range(GROUP):
            raise_up(m, k, top)
            if m + 1 < TEAM:
                score(m + 1, k)
        if m + 1 < TEAM:
            turn(m + GROUP)
        scale = 1.0 / jnp.sum(sums[m][0], axis=0, keepdims=True)
        delta = jnp.sum(sums[m][1], axis=0, keepdims=True) * scale
        for k in range(GROUP):
            settle(m, k, scale, delta)
            if m and k == 1:
                query_side(m - 1)
            if m and k == 4:
                key_side(m - 1)
    query_side(TEAM - 1)
    for w in range(TEAM - 1, HALO + TEAM):
        key_side(w)


def attention(kind, *operands):
    def kernel(*refs):
        attention_kernel(kind, *refs)

    return pl.pallas_call(
        kernel,
        out_shape=(
            block_shape(TEAM),
            block_shape(TEAM, dtype=jnp.float32),
            block_shape(HALO),
        ),
        in_specs=smem() + vmem(len(operands) - 1),
        out_specs=tuple(vmem(3)),
        scratch_shapes=[
            pltpu.VMEM((PAIR, SPAN), jnp.bfloat16),
            pltpu.VMEM((2, GROUP, ROWS, BOTH), jnp.float32),
            pltpu.VMEM((SPAN, TEAM * BOTH), jnp.bfloat16),
            pltpu.VMEM((TEAM * BOTH, PAIR), jnp.bfloat16),
        ],
        compiler_params=pltpu.CompilerParams(vmem_limit_bytes=VMEM_BYTES),
        cost_estimate=pl.CostEstimate(flops=0, bytes_accessed=0, transcendentals=0),
        name="attention_cross" if kind == CROSS else "attention_self",
    )(*operands)


def join_kernel(own_s, own_c, home_s, home_c, out_s, out_c, out):
    for kind, own, home in ((SELF, own_s, home_s), (CROSS, own_c, home_c)):
        out[0, kind] = own[0].astype(jnp.bfloat16)
        for b in range(HALO):
            out[b + 1, kind] = (own[b + 1] + home[b].astype(jnp.float32)).astype(jnp.bfloat16)
    for b in range(TEAM):
        out[b, NEAR] = out_s[b]
        out[b, FAR] = out_c[b]


def halves(first, second):
    left = jnp.concatenate([first[:, :HEAD], second[:, :HEAD]], axis=1)
    right = jnp.concatenate([first[:, HEAD:], second[:, HEAD:]], axis=1)
    return left, right


def unpack_kernel(parts, attended, query_s, key_s, value_s, query_c, key_c, value_c):
    flip = my_flip()
    for h in range(0, HEADS, 2):
        lanes = pl.ds(h * HEAD, PAIR)
        first, second = parts.at[jnp.bitwise_xor(h, flip)], parts.at[jnp.bitwise_xor(h + 1, flip)]
        key_s[:, lanes], value_s[:, lanes] = halves(first[SELF], second[SELF])
        key_c[:, lanes], value_c[:, lanes] = halves(first[CROSS], second[CROSS])
        query_s[:, lanes], near = halves(first[NEAR], second[NEAR])
        query_c[:, lanes], far = halves(first[FAR], second[FAR])
        total = near.astype(jnp.float32) + far.astype(jnp.float32)
        attended[:, lanes] = total.astype(jnp.bfloat16)


def local_call(kernel, out_shape, in_specs, operands, name, scratch=()):
    return pl.pallas_call(
        kernel,
        out_shape=out_shape,
        in_specs=in_specs,
        out_specs=jax.tree.map(lambda shape: vmem(1)[0], out_shape),
        scratch_shapes=scratch,
        compiler_params=pltpu.CompilerParams(vmem_limit_bytes=VMEM_BYTES),
        cost_estimate=pl.CostEstimate(flops=0, bytes_accessed=0, transcendentals=0),
        name=name,
    )(*operands)


def to_next_team(value, step):
    count = lax.axis_size("ctx")
    route = [(i, (i + step * TEAM) % count ^ (TEAM // 2)) for i in range(count)]
    return lax.ppermute(value, "ctx", route)


def within_team(value):
    count = lax.axis_size("ctx")
    teams = [list(range(at, at + TEAM)) for at in range(0, count, TEAM)]
    return lax.all_to_all(value, "ctx", 0, 0, axis_index_groups=teams, tiled=True)


def swapped(value):
    return lax.ppermute(value, "tower", [(0, 1), (1, 0)])


def body(
    query_self, key_self, value_self, query_cross, key_cross, value_cross, cotangent, block_slot
):
    count = lax.axis_size("ctx")
    member = lax.rem(lax.axis_index("ctx"), TEAM)
    slots = jnp.stack([lax.rem(block_slot[0] - member + count, count), jnp.int32(count)])
    flat = jax.ShapeDtypeStruct((ROWS, FEATURES), jnp.bfloat16)
    inputs = (query_self, key_self, value_self, query_cross, key_cross, value_cross, cotangent)
    far, near = local_call(
        pack_kernel,
        (block_shape(TEAM), block_shape(TEAM, 3)),
        [pl.BlockSpec(memory_space=pltpu.HBM)] * 7,
        tuple(pltpu.with_memory_space_constraint(value[0], pltpu.HBM) for value in inputs),
        "pack",
        [pltpu.VMEM((7, ROWS, FEATURES), jnp.bfloat16), pltpu.SemaphoreType.DMA((7,))],
    )
    arrived = swapped(far)
    own = within_team(near)
    halo = to_next_team(own[1:, :NEAR], 1)
    crossing = within_team(arrived)
    out_s, own_s, back_s = attention(SELF, slots, own, halo)
    out_c, own_c, back_c = attention(CROSS, slots, crossing, own, halo)
    home_s = to_next_team(back_s, -1)
    home_c = to_next_team(back_c, -1)
    joined = local_call(
        join_kernel,
        block_shape(TEAM, 4),
        vmem(6),
        (own_s, own_c, home_s, home_c, out_s, swapped(out_c)),
        "join",
    )
    outs = local_call(unpack_kernel, (flat,) * 7, vmem(1), (within_team(joined),), "unpack")
    return tuple(part[None] for part in outs)


def solution(mesh):
    rows = P("tower", ("dp", "ctx"), None)
    return jax.shard_map(
        body,
        mesh=mesh,
        in_specs=(rows,) * 7 + (P("ctx"),),
        out_specs=(rows,) * 7,
        check_vma=False,
    )
```

```python
import jax
import jax.numpy as jnp
from jax import lax
from jax.experimental import pallas as pl
from jax.experimental.pallas import tpu as pltpu
from jax.sharding import PartitionSpec as P

HEADS = 8
HEAD = 64
ROWS = 128
GROUP = 8
TEAM = 8
PAIR = 2 * HEAD
BOTH = 2 * ROWS
HALO = GROUP - 1
WINDOW = GROUP * ROWS
SPAN = (HALO + TEAM) * ROWS
FEATURES = HEADS * HEAD
VMEM_BYTES = 48 * 1024 * 1024
SELF, CROSS, NEAR, FAR = 0, 1, 2, 3


def vmem(count):
    return [pl.BlockSpec(memory_space=pltpu.VMEM)] * count


def smem():
    return [pl.BlockSpec(memory_space=pltpu.SMEM)]


def block_shape(*lead, dtype=jnp.bfloat16):
    return jax.ShapeDtypeStruct((*lead, ROWS, PAIR), dtype)


def paired(left, right, h):
    lanes = pl.ds(h * HEAD, HEAD)
    return jnp.concatenate([left[:, lanes], right[:, lanes]], axis=1)


def my_flip():
    return lax.rem(lax.axis_index("ctx") // TEAM, 2) * (TEAM // 2)


def pack_kernel(
    query_s, key_s, value_s, query_c, key_c, value_c, upstream, far, near, held, arrived
):
    sources = (upstream, query_c, query_s, key_s, value_s, key_c, value_c)
    copies = [
        pltpu.make_async_copy(source, held.at[i], arrived.at[i])
        for i, source in enumerate(sources)
    ]
    for copy in copies:
        copy.start()
    flip = my_flip()
    copies[0].wait()
    for kind, left, right in ((FAR, 1, 0), (NEAR, 2, 0), (SELF, 3, 4), (CROSS, 5, 6)):
        copies[left].wait()
        if right:
            copies[right].wait()
        for h in range(HEADS):
            value = paired(held.at[left], held.at[right], h)
            if kind == FAR:
                far[jnp.bitwise_xor(h, flip)] = value
            else:
                near[jnp.bitwise_xor(h, flip), kind] = value


def attention_kernel(kind, slots, *refs):
    if kind == SELF:
        own, edge, out, dkv_own, dkv_halo, kv_t, scores, probs, stacks = refs
        queries = [own.at[b, NEAR] for b in range(TEAM)]
    else:
        qdo, own, plane, below, out, dkv_own, dkv_halo, kv_t, scores, probs, stacks, edge = refs
        queries = [qdo.at[b] for b in range(TEAM)]

        @pl.when(my_flip() == 0)
        def _():
            edge[...] = below[...]

        @pl.when(my_flip() != 0)
        def _():
            edge[...] = plane[...]

    blocks = [edge.at[b] for b in range(HALO)] + [own.at[b, kind] for b in range(TEAM)]
    first_half = lax.broadcasted_iota(jnp.int32, (ROWS, PAIR), 1) < HEAD
    causal = lax.broadcasted_iota(jnp.int32, (ROWS, ROWS), 0) <= lax.broadcasted_iota(
        jnp.int32, (ROWS, ROWS), 1
    )
    peaks, hidden, sums = {}, {}, {}

    def turn(w):
        kv_t[:, w * ROWS : (w + 1) * ROWS] = blocks[w][...].T

    def begin(m):
        both = queries[m][...]
        none = jnp.zeros_like(both)
        stacks[m * BOTH : m * BOTH + ROWS, :] = jnp.where(
            first_half, both * jnp.bfloat16(HEAD ** (-0.5)), none
        )
        stacks[m * BOTH + ROWS : (m + 1) * BOTH, :] = jnp.where(first_half, none, both)
        slot = lax.rem(slots[0] + m, slots[1])
        hidden[m] = [jnp.where(slot >= HALO - k, 0.0, 1e30) for k in range(HALO)] + [0.0]

    def score(m, k):
        part = lax.dot_general(
            blocks[m + k][...],
            stacks[m * BOTH : (m + 1) * BOTH, :],
            (((1,), (1,)), ((), ())),
            preferred_element_type=jnp.float32,
        )
        logits = part[:, :ROWS]
        if k == GROUP - 1:
            logits = jnp.where(causal, logits, -1e30)
        scores[m % 2, k, :, :ROWS] = logits
        scores[m % 2, k, :, ROWS:] = part[:, ROWS:]
        peak = jnp.max(logits.reshape(ROWS // 8, 8, ROWS), axis=0) - hidden[m][k]
        peaks[m] = peak if k == 0 else jnp.maximum(peaks[m], peak)

    def raise_up(m, k, top):
        raised = jnp.exp(scores[m % 2, k, :, :ROWS] - (top + hidden[m][k]))
        change = raised * scores[m % 2, k, :, ROWS:]
        scores[m % 2, k, :, :ROWS] = raised
        total = jnp.sum(raised.reshape(ROWS // 8, 8, ROWS), axis=0)
        weighted = jnp.sum(change.reshape(ROWS // 8, 8, ROWS), axis=0)
        sums[m] = (total, weighted) if k == 0 else (sums[m][0] + total, sums[m][1] + weighted)

    def settle(m, k, scale, delta):
        weight = scores[m % 2, k, :, :ROWS] * scale
        change = weight * (scores[m % 2, k, :, ROWS:] - delta)
        rows, lanes = slice((m + k) * ROWS, (m + k + 1) * ROWS), m * BOTH
        probs[rows, lanes : lanes + ROWS] = change.astype(jnp.bfloat16)
        probs[rows, lanes + ROWS : lanes + BOTH] = weight.astype(jnp.bfloat16)

    def query_side(m):
        window, lanes = slice(m * ROWS, m * ROWS + WINDOW), m * BOTH
        mixed = lax.dot_general(
            kv_t[:, window],
            probs[window, lanes : lanes + BOTH],
            (((1,), (0,)), ((), ())),
            preferred_element_type=jnp.float32,
        )
        result = jnp.concatenate(
            [mixed[:HEAD, :ROWS] * HEAD ** (-0.5), mixed[HEAD:, ROWS:]], axis=0
        )
        out[m] = result.T.astype(jnp.bfloat16)

    def key_side(w):
        low, high = max(0, w - HALO), min(TEAM - 1, w) + 1
        total = lax.dot_general(
            probs[w * ROWS : (w + 1) * ROWS, low * BOTH : high * BOTH],
            stacks[low * BOTH : high * BOTH, :],
            (((1,), (0,)), ((), ())),
            preferred_element_type=jnp.float32,
        )
        if w < HALO:
            dkv_halo[w] = total.astype(jnp.bfloat16)
        else:
            dkv_own[w - HALO] = total

    begin(0)
    for k in range(GROUP):
        score(0, k)
        turn(k)
    for m in range(TEAM):
        top = jnp.max(peaks[m], axis=0, keepdims=True)
        if m + 1 < TEAM:
            begin(m + 1)
        for k in range(GROUP):
            raise_up(m, k, top)
            if m + 1 < TEAM:
                score(m + 1, k)
        if m + 1 < TEAM:
            turn(m + GROUP)
        scale = 1.0 / jnp.sum(sums[m][0], axis=0, keepdims=True)
        delta = jnp.sum(sums[m][1], axis=0, keepdims=True) * scale
        for k in range(GROUP):
            settle(m, k, scale, delta)
            if m and k == 1:
                query_side(m - 1)
            if m and k == 4:
                key_side(m - 1)
    query_side(TEAM - 1)
    for w in range(TEAM - 1, HALO + TEAM):
        key_side(w)


def attention(kind, *operands):
    def kernel(*refs):
        attention_kernel(kind, *refs)

    return pl.pallas_call(
        kernel,
        out_shape=(
            block_shape(TEAM),
            block_shape(TEAM, dtype=jnp.float32),
            block_shape(HALO),
        ),
        in_specs=smem() + vmem(len(operands) - 1),
        out_specs=tuple(vmem(3)),
        scratch_shapes=[
            pltpu.VMEM((PAIR, SPAN), jnp.bfloat16),
            pltpu.VMEM((2, GROUP, ROWS, BOTH), jnp.float32),
            pltpu.VMEM((SPAN, TEAM * BOTH), jnp.bfloat16),
            pltpu.VMEM((TEAM * BOTH, PAIR), jnp.bfloat16),
        ]
        + [pltpu.VMEM((HALO, ROWS, PAIR), jnp.bfloat16)] * (kind == CROSS),
        compiler_params=pltpu.CompilerParams(vmem_limit_bytes=VMEM_BYTES),
        cost_estimate=pl.CostEstimate(flops=0, bytes_accessed=0, transcendentals=0),
        name="attention_cross" if kind == CROSS else "attention_self",
    )(*operands)


def join_kernel(own_s, own_c, home_s, plane, above, out_s, out_c, out):
    def add(kind, own, home):
        out[0, kind] = own[0].astype(jnp.bfloat16)
        for b in range(HALO):
            out[b + 1, kind] = (own[b + 1] + home[b].astype(jnp.float32)).astype(jnp.bfloat16)

    add(SELF, own_s, home_s)

    @pl.when(my_flip() == 0)
    def _():
        add(CROSS, own_c, plane)

    @pl.when(my_flip() != 0)
    def _():
        add(CROSS, own_c, above)

    for b in range(TEAM):
        out[b, NEAR] = out_s[b]
        out[b, FAR] = out_c[b]


def halves(first, second):
    left = jnp.concatenate([first[:, :HEAD], second[:, :HEAD]], axis=1)
    right = jnp.concatenate([first[:, HEAD:], second[:, HEAD:]], axis=1)
    return left, right


def unpack_kernel(parts, attended, query_s, key_s, value_s, query_c, key_c, value_c):
    flip = my_flip()
    for h in range(0, HEADS, 2):
        lanes = pl.ds(h * HEAD, PAIR)
        first, second = parts.at[jnp.bitwise_xor(h, flip)], parts.at[jnp.bitwise_xor(h + 1, flip)]
        key_s[:, lanes], value_s[:, lanes] = halves(first[SELF], second[SELF])
        key_c[:, lanes], value_c[:, lanes] = halves(first[CROSS], second[CROSS])
        query_s[:, lanes], near = halves(first[NEAR], second[NEAR])
        query_c[:, lanes], far = halves(first[FAR], second[FAR])
        total = near.astype(jnp.float32) + far.astype(jnp.float32)
        attended[:, lanes] = total.astype(jnp.bfloat16)


def local_call(kernel, out_shape, in_specs, operands, name, scratch=()):
    return pl.pallas_call(
        kernel,
        out_shape=out_shape,
        in_specs=in_specs,
        out_specs=jax.tree.map(lambda shape: vmem(1)[0], out_shape),
        scratch_shapes=scratch,
        compiler_params=pltpu.CompilerParams(vmem_limit_bytes=VMEM_BYTES),
        cost_estimate=pl.CostEstimate(flops=0, bytes_accessed=0, transcendentals=0),
        name=name,
    )(*operands)


def to_next_team(value, step):
    count = lax.axis_size("ctx")
    route = [(i, (i + step * TEAM) % count ^ (TEAM // 2)) for i in range(count)]
    return lax.ppermute(value, "ctx", route)


def in_plane(value):
    count = lax.axis_size("ctx")
    return lax.ppermute(value, "ctx", [(i, i ^ (TEAM + TEAM // 2)) for i in range(count)])


def to_next_plane(value, step, odd):
    count = lax.axis_size("ctx")
    senders = [i for i in range(count) if i // TEAM % 2 == odd]
    return lax.ppermute(value, "ctx", [(i, (i + step * 2 * TEAM) % count) for i in senders])


def within_team(value):
    count = lax.axis_size("ctx")
    teams = [list(range(at, at + TEAM)) for at in range(0, count, TEAM)]
    return lax.all_to_all(value, "ctx", 0, 0, axis_index_groups=teams, tiled=True)


def swapped(value):
    return lax.ppermute(value, "tower", [(0, 1), (1, 0)])


def body(
    query_self, key_self, value_self, query_cross, key_cross, value_cross, cotangent, block_slot
):
    count = lax.axis_size("ctx")
    member = lax.rem(lax.axis_index("ctx"), TEAM)
    slots = jnp.stack([lax.rem(block_slot[0] - member + count, count), jnp.int32(count)])
    flat = jax.ShapeDtypeStruct((ROWS, FEATURES), jnp.bfloat16)
    inputs = (query_self, key_self, value_self, query_cross, key_cross, value_cross, cotangent)
    far, near = local_call(
        pack_kernel,
        (block_shape(TEAM), block_shape(TEAM, 3)),
        [pl.BlockSpec(memory_space=pltpu.HBM)] * 7,
        tuple(pltpu.with_memory_space_constraint(value[0], pltpu.HBM) for value in inputs),
        "pack",
        [pltpu.VMEM((7, ROWS, FEATURES), jnp.bfloat16), pltpu.SemaphoreType.DMA((7,))],
    )
    arrived = swapped(far)
    own = within_team(near)
    halo = to_next_team(own[1:, SELF], 1)
    plane = in_plane(own[1:, CROSS])
    below = to_next_plane(plane, 1, 0)
    crossing = within_team(arrived)
    out_s, own_s, back_s = attention(SELF, slots, own, halo)
    out_c, own_c, back_c = attention(CROSS, slots, crossing, own, plane, below)
    home_s = to_next_team(back_s, -1)
    home_c = in_plane(back_c)
    above = to_next_plane(home_c, -1, 1)
    joined = local_call(
        join_kernel,
        block_shape(TEAM, 4),
        vmem(7),
        (own_s, own_c, home_s, home_c, above, out_s, swapped(out_c)),
        "join",
    )
    outs = local_call(unpack_kernel, (flat,) * 7, vmem(1), (within_team(joined),), "unpack")
    return tuple(part[None] for part in outs)


def solution(mesh):
    rows = P("tower", ("dp", "ctx"), None)
    return jax.shard_map(
        body,
        mesh=mesh,
        in_specs=(rows,) * 7 + (P("ctx"),),
        out_specs=(rows,) * 7,
        check_vma=False,
    )
```

```python
import jax
import jax.numpy as jnp
from jax import lax
from jax.experimental import pallas as pl
from jax.experimental.pallas import tpu as pltpu
from jax.sharding import PartitionSpec as P

HEADS = 8
HEAD = 64
ROWS = 128
GROUP = 8
TEAM = 8
PAIR = 2 * HEAD
BOTH = 2 * ROWS
HALO = GROUP - 1
WINDOW = GROUP * ROWS
SPAN = (HALO + TEAM) * ROWS
FEATURES = HEADS * HEAD
VMEM_BYTES = 48 * 1024 * 1024
SELF, CROSS, NEAR, FAR = 0, 1, 2, 3


def vmem(count):
    return [pl.BlockSpec(memory_space=pltpu.VMEM)] * count


def smem():
    return [pl.BlockSpec(memory_space=pltpu.SMEM)]


def block_shape(*lead, dtype=jnp.bfloat16):
    return jax.ShapeDtypeStruct((*lead, ROWS, PAIR), dtype)


def paired(left, right, h):
    lanes = pl.ds(h * HEAD, HEAD)
    return jnp.concatenate([left[:, lanes], right[:, lanes]], axis=1)


def my_flip():
    return lax.rem(lax.axis_index("ctx") // TEAM, 2) * (TEAM // 2)


def pack_kernel(
    query_s, key_s, value_s, query_c, key_c, value_c, upstream, far, near, held, arrived
):
    sources = (upstream, query_c, query_s, key_s, value_s, key_c, value_c)
    copies = [
        pltpu.make_async_copy(source, held.at[i], arrived.at[i])
        for i, source in enumerate(sources)
    ]
    for copy in copies:
        copy.start()
    flip = my_flip()
    copies[0].wait()
    for kind, left, right in ((FAR, 1, 0), (NEAR, 2, 0), (SELF, 3, 4), (CROSS, 5, 6)):
        copies[left].wait()
        if right:
            copies[right].wait()
        for h in range(HEADS):
            value = paired(held.at[left], held.at[right], h)
            if kind == FAR:
                far[jnp.bitwise_xor(h, flip)] = value
            else:
                near[jnp.bitwise_xor(h, flip), kind] = value


def attention_kernel(kind, slots, *refs):
    if kind == SELF:
        own, halo, out, dkv_own, dkv_halo, kv_t, scores, probs, stacks = refs
        queries = [own.at[b, NEAR] for b in range(TEAM)]
    else:
        qdo, own, halo, out, dkv_own, dkv_halo, kv_t, scores, probs, stacks = refs
        queries = [qdo.at[b] for b in range(TEAM)]
    blocks = [halo.at[b] for b in range(HALO)] + [own.at[b, kind] for b in range(TEAM)]
    first_half = lax.broadcasted_iota(jnp.int32, (ROWS, PAIR), 1) < HEAD
    causal = lax.broadcasted_iota(jnp.int32, (ROWS, ROWS), 0) <= lax.broadcasted_iota(
        jnp.int32, (ROWS, ROWS), 1
    )
    peaks, hidden, sums = {}, {}, {}

    def turn(w):
        kv_t[:, w * ROWS : (w + 1) * ROWS] = blocks[w][...].T

    def begin(m):
        both = queries[m][...]
        none = jnp.zeros_like(both)
        stacks[m * BOTH : m * BOTH + ROWS, :] = jnp.where(
            first_half, both * jnp.bfloat16(HEAD ** (-0.5)), none
        )
        stacks[m * BOTH + ROWS : (m + 1) * BOTH, :] = jnp.where(first_half, none, both)
        slot = lax.rem(slots[0] + m, slots[1])
        hidden[m] = [jnp.where(slot >= HALO - k, 0.0, 1e30) for k in range(HALO)] + [0.0]

    def score(m, k):
        part = lax.dot_general(
            blocks[m + k][...],
            stacks[m * BOTH : (m + 1) * BOTH, :],
            (((1,), (1,)), ((), ())),
            preferred_element_type=jnp.float32,
        )
        logits = part[:, :ROWS]
        if k == GROUP - 1:
            logits = jnp.where(causal, logits, -1e30)
        scores[m % 2, k, :, :ROWS] = logits
        scores[m % 2, k, :, ROWS:] = part[:, ROWS:]
        peak = jnp.max(logits.reshape(ROWS // 8, 8, ROWS), axis=0) - hidden[m][k]
        peaks[m] = peak if k == 0 else jnp.maximum(peaks[m], peak)

    def raise_up(m, k, top):
        raised = jnp.exp(scores[m % 2, k, :, :ROWS] - (top + hidden[m][k]))
        change = raised * scores[m % 2, k, :, ROWS:]
        scores[m % 2, k, :, :ROWS] = raised
        total = jnp.sum(raised.reshape(ROWS // 8, 8, ROWS), axis=0)
        weighted = jnp.sum(change.reshape(ROWS // 8, 8, ROWS), axis=0)
        sums[m] = (total, weighted) if k == 0 else (sums[m][0] + total, sums[m][1] + weighted)

    def settle(m, k, scale, delta):
        weight = scores[m % 2, k, :, :ROWS] * scale
        change = weight * (scores[m % 2, k, :, ROWS:] - delta)
        rows, lanes = slice((m + k) * ROWS, (m + k + 1) * ROWS), m * BOTH
        probs[rows, lanes : lanes + ROWS] = change.astype(jnp.bfloat16)
        probs[rows, lanes + ROWS : lanes + BOTH] = weight.astype(jnp.bfloat16)

    def query_side(m):
        window, lanes = slice(m * ROWS, m * ROWS + WINDOW), m * BOTH
        mixed = lax.dot_general(
            kv_t[:, window],
            probs[window, lanes : lanes + BOTH],
            (((1,), (0,)), ((), ())),
            preferred_element_type=jnp.float32,
        )
        result = jnp.concatenate(
            [mixed[:HEAD, :ROWS] * HEAD ** (-0.5), mixed[HEAD:, ROWS:]], axis=0
        )
        out[m] = result.T.astype(jnp.bfloat16)

    def key_side(w):
        low, high = max(0, w - HALO), min(TEAM - 1, w) + 1
        total = lax.dot_general(
            probs[w * ROWS : (w + 1) * ROWS, low * BOTH : high * BOTH],
            stacks[low * BOTH : high * BOTH, :],
            (((1,), (0,)), ((), ())),
            preferred_element_type=jnp.float32,
        )
        if w < HALO:
            dkv_halo[w] = total.astype(jnp.bfloat16)
        else:
            dkv_own[w - HALO] = total

    begin(0)
    for k in range(GROUP):
        score(0, k)
        turn(k)
    for m in range(TEAM):
        top = jnp.max(peaks[m], axis=0, keepdims=True)
        if m + 1 < TEAM:
            begin(m + 1)
        for k in range(GROUP):
            raise_up(m, k, top)
            if m + 1 < TEAM:
                score(m + 1, k)
        if m + 1 < TEAM:
            turn(m + GROUP)
        scale = 1.0 / jnp.sum(sums[m][0], axis=0, keepdims=True)
        delta = jnp.sum(sums[m][1], axis=0, keepdims=True) * scale
        for k in range(GROUP):
            settle(m, k, scale, delta)
            if m and k == 1:
                query_side(m - 1)
            if m and k == 4:
                key_side(m - 1)
    query_side(TEAM - 1)
    for w in range(TEAM - 1, HALO + TEAM):
        key_side(w)


def attention(kind, *operands):
    def kernel(*refs):
        attention_kernel(kind, *refs)

    return pl.pallas_call(
        kernel,
        out_shape=(
            block_shape(TEAM),
            block_shape(TEAM, dtype=jnp.float32),
            block_shape(HALO),
        ),
        in_specs=smem() + vmem(len(operands) - 1),
        out_specs=tuple(vmem(3)),
        scratch_shapes=[
            pltpu.VMEM((PAIR, SPAN), jnp.bfloat16),
            pltpu.VMEM((2, GROUP, ROWS, BOTH), jnp.float32),
            pltpu.VMEM((SPAN, TEAM * BOTH), jnp.bfloat16),
            pltpu.VMEM((TEAM * BOTH, PAIR), jnp.bfloat16),
        ],
        compiler_params=pltpu.CompilerParams(vmem_limit_bytes=VMEM_BYTES),
        cost_estimate=pl.CostEstimate(flops=0, bytes_accessed=0, transcendentals=0),
        name="attention_cross" if kind == CROSS else "attention_self",
    )(*operands)


def join_kernel(own_s, own_c, home_s, home_c, out_c, out):
    for kind, own, home in ((SELF, own_s, home_s), (CROSS, own_c, home_c)):
        out[0, kind] = own[0].astype(jnp.bfloat16)
        for b in range(HALO):
            out[b + 1, kind] = (own[b + 1] + home[b].astype(jnp.float32)).astype(jnp.bfloat16)
    for b in range(TEAM):
        out[b, NEAR] = out_c[b]


def halves(first, second):
    left = jnp.concatenate([first[:, :HEAD], second[:, :HEAD]], axis=1)
    right = jnp.concatenate([first[:, HEAD:], second[:, HEAD:]], axis=1)
    return left, right


def unpack_kernel(parts, parts_s, attended, query_s, key_s, value_s, query_c, key_c, value_c):
    flip = my_flip()
    for h in range(0, HEADS, 2):
        lanes = pl.ds(h * HEAD, PAIR)
        left, right = jnp.bitwise_xor(h, flip), jnp.bitwise_xor(h + 1, flip)
        first, second = parts.at[left], parts.at[right]
        key_s[:, lanes], value_s[:, lanes] = halves(first[SELF], second[SELF])
        key_c[:, lanes], value_c[:, lanes] = halves(first[CROSS], second[CROSS])
        query_s[:, lanes], near = halves(parts_s[left], parts_s[right])
        query_c[:, lanes], far = halves(first[NEAR], second[NEAR])
        total = near.astype(jnp.float32) + far.astype(jnp.float32)
        attended[:, lanes] = total.astype(jnp.bfloat16)


def local_call(kernel, out_shape, in_specs, operands, name, scratch=()):
    return pl.pallas_call(
        kernel,
        out_shape=out_shape,
        in_specs=in_specs,
        out_specs=jax.tree.map(lambda shape: vmem(1)[0], out_shape),
        scratch_shapes=scratch,
        compiler_params=pltpu.CompilerParams(vmem_limit_bytes=VMEM_BYTES),
        cost_estimate=pl.CostEstimate(flops=0, bytes_accessed=0, transcendentals=0),
        name=name,
    )(*operands)


def to_next_team(value, step):
    count = lax.axis_size("ctx")
    route = [(i, (i + step * TEAM) % count ^ (TEAM // 2)) for i in range(count)]
    return lax.ppermute(value, "ctx", route)


def within_team(value):
    count = lax.axis_size("ctx")
    teams = [list(range(at, at + TEAM)) for at in range(0, count, TEAM)]
    return lax.all_to_all(value, "ctx", 0, 0, axis_index_groups=teams, tiled=True)


def swapped(value):
    return lax.ppermute(value, "tower", [(0, 1), (1, 0)])


def body(
    query_self, key_self, value_self, query_cross, key_cross, value_cross, cotangent, block_slot
):
    count = lax.axis_size("ctx")
    member = lax.rem(lax.axis_index("ctx"), TEAM)
    slots = jnp.stack([lax.rem(block_slot[0] - member + count, count), jnp.int32(count)])
    flat = jax.ShapeDtypeStruct((ROWS, FEATURES), jnp.bfloat16)
    inputs = (query_self, key_self, value_self, query_cross, key_cross, value_cross, cotangent)
    far, near = local_call(
        pack_kernel,
        (block_shape(TEAM), block_shape(TEAM, 3)),
        [pl.BlockSpec(memory_space=pltpu.HBM)] * 7,
        tuple(pltpu.with_memory_space_constraint(value[0], pltpu.HBM) for value in inputs),
        "pack",
        [pltpu.VMEM((7, ROWS, FEATURES), jnp.bfloat16), pltpu.SemaphoreType.DMA((7,))],
    )
    arrived = swapped(far)
    own = within_team(near)
    halo_c = to_next_team(own[1:, CROSS], 1)
    halo_s = to_next_team(own[1:, SELF], 1)
    crossing = within_team(arrived)
    out_s, own_s, back_s = attention(SELF, slots, own, halo_s)
    out_c, own_c, back_c = attention(CROSS, slots, crossing, own, halo_c)
    home_s = to_next_team(back_s, -1)
    home_c = to_next_team(back_c, -1)
    joined = local_call(
        join_kernel,
        block_shape(TEAM, 3),
        vmem(5),
        (own_s, own_c, home_s, home_c, swapped(out_c)),
        "join",
    )
    parts_s = within_team(out_s)
    outs = local_call(
        unpack_kernel, (flat,) * 7, vmem(2), (within_team(joined), parts_s), "unpack"
    )
    return tuple(part[None] for part in outs)


def solution(mesh):
    rows = P("tower", ("dp", "ctx"), None)
    return jax.shard_map(
        body,
        mesh=mesh,
        in_specs=(rows,) * 7 + (P("ctx"),),
        out_specs=(rows,) * 7,
        check_vma=False,
    )
```

```python
import jax
import jax.numpy as jnp
from jax import lax
from jax.experimental import pallas as pl
from jax.experimental.pallas import tpu as pltpu
from jax.sharding import PartitionSpec as P

HEADS = 8
HEAD = 64
ROWS = 128
GROUP = 8
TEAM = 8
PAIR = 2 * HEAD
BOTH = 2 * ROWS
HALO = GROUP - 1
WINDOW = GROUP * ROWS
SPAN = (HALO + TEAM) * ROWS
FEATURES = HEADS * HEAD
VMEM_BYTES = 48 * 1024 * 1024
SELF, CROSS, NEAR, FAR = 0, 1, 2, 3


def vmem(count):
    return [pl.BlockSpec(memory_space=pltpu.VMEM)] * count


def smem():
    return [pl.BlockSpec(memory_space=pltpu.SMEM)]


def block_shape(*lead, dtype=jnp.bfloat16):
    return jax.ShapeDtypeStruct((*lead, ROWS, PAIR), dtype)


def paired(left, right, h):
    lanes = pl.ds(h * HEAD, HEAD)
    return jnp.concatenate([left[:, lanes], right[:, lanes]], axis=1)


def my_flip():
    return lax.rem(lax.axis_index("ctx") // TEAM, 2) * (TEAM // 2)


def pack_kernel(
    query_s, key_s, value_s, query_c, key_c, value_c, upstream, far, near, held, arrived
):
    sources = (upstream, query_c, query_s, key_s, value_s, key_c, value_c)
    copies = [
        pltpu.make_async_copy(source, held.at[i], arrived.at[i])
        for i, source in enumerate(sources)
    ]
    for copy in copies:
        copy.start()
    flip = my_flip()
    copies[0].wait()
    for kind, left, right in ((FAR, 1, 0), (NEAR, 2, 0), (SELF, 3, 4), (CROSS, 5, 6)):
        copies[left].wait()
        if right:
            copies[right].wait()
        for h in range(HEADS):
            value = paired(held.at[left], held.at[right], h)
            if kind == FAR:
                far[jnp.bitwise_xor(h, flip)] = value
            else:
                near[jnp.bitwise_xor(h, flip), kind] = value


def attention_kernel(kind, slots, *refs):
    if kind == SELF:
        own, halo, out, dkv_own, dkv_halo, kv_t, scores, probs, stacks = refs
        queries = [own.at[b, NEAR] for b in range(TEAM)]
    else:
        qdo, own, halo, out, dkv_own, dkv_halo, kv_t, scores, probs, stacks = refs
        queries = [qdo.at[b] for b in range(TEAM)]
    blocks = [halo.at[b, kind] for b in range(HALO)] + [own.at[b, kind] for b in range(TEAM)]
    first_half = lax.broadcasted_iota(jnp.int32, (ROWS, PAIR), 1) < HEAD
    causal = lax.broadcasted_iota(jnp.int32, (ROWS, ROWS), 0) <= lax.broadcasted_iota(
        jnp.int32, (ROWS, ROWS), 1
    )
    peaks, hidden, sums = {}, {}, {}

    def turn(w):
        kv_t[:, w * ROWS : (w + 1) * ROWS] = blocks[w][...].T

    def begin(m):
        both = queries[m][...]
        none = jnp.zeros_like(both)
        stacks[m * BOTH : m * BOTH + ROWS, :] = jnp.where(
            first_half, both * jnp.bfloat16(HEAD ** (-0.5)), none
        )
        stacks[m * BOTH + ROWS : (m + 1) * BOTH, :] = jnp.where(first_half, none, both)
        slot = lax.rem(slots[0] + m, slots[1])
        hidden[m] = [jnp.where(slot >= HALO - k, 0.0, 1e30) for k in range(HALO)] + [0.0]

    def score(m, k):
        part = lax.dot_general(
            blocks[m + k][...],
            stacks[m * BOTH : (m + 1) * BOTH, :],
            (((1,), (1,)), ((), ())),
            preferred_element_type=jnp.float32,
        )
        logits = part[:, :ROWS]
        if k == GROUP - 1:
            logits = jnp.where(causal, logits, -1e30)
        scores[m % 2, k, :, :ROWS] = logits
        scores[m % 2, k, :, ROWS:] = part[:, ROWS:]
        peak = jnp.max(logits.reshape(ROWS // 8, 8, ROWS), axis=0) - hidden[m][k]
        peaks[m] = peak if k == 0 else jnp.maximum(peaks[m], peak)

    def raise_up(m, k, top):
        raised = jnp.exp(scores[m % 2, k, :, :ROWS] - (top + hidden[m][k]))
        change = raised * scores[m % 2, k, :, ROWS:]
        scores[m % 2, k, :, :ROWS] = raised
        total = jnp.sum(raised.reshape(ROWS // 8, 8, ROWS), axis=0)
        weighted = jnp.sum(change.reshape(ROWS // 8, 8, ROWS), axis=0)
        sums[m] = (total, weighted) if k == 0 else (sums[m][0] + total, sums[m][1] + weighted)

    def settle(m, k, scale, delta):
        weight = scores[m % 2, k, :, :ROWS] * scale
        change = weight * (scores[m % 2, k, :, ROWS:] - delta)
        rows, lanes = slice((m + k) * ROWS, (m + k + 1) * ROWS), m * BOTH
        probs[rows, lanes : lanes + ROWS] = change.astype(jnp.bfloat16)
        probs[rows, lanes + ROWS : lanes + BOTH] = weight.astype(jnp.bfloat16)

    def query_side(m):
        window, lanes = slice(m * ROWS, m * ROWS + WINDOW), m * BOTH
        mixed = lax.dot_general(
            kv_t[:, window],
            probs[window, lanes : lanes + BOTH],
            (((1,), (0,)), ((), ())),
            preferred_element_type=jnp.float32,
        )
        result = jnp.concatenate(
            [mixed[:HEAD, :ROWS] * HEAD ** (-0.5), mixed[HEAD:, ROWS:]], axis=0
        )
        out[m] = result.T.astype(jnp.bfloat16)

    def key_side(w):
        low, high = max(0, w - HALO), min(TEAM - 1, w) + 1
        total = lax.dot_general(
            probs[w * ROWS : (w + 1) * ROWS, low * BOTH : high * BOTH],
            stacks[low * BOTH : high * BOTH, :],
            (((1,), (0,)), ((), ())),
            preferred_element_type=jnp.float32,
        )
        if w < HALO:
            dkv_halo[w] = total.astype(jnp.bfloat16)
        else:
            dkv_own[w - HALO] = total

    begin(0)
    for k in range(GROUP):
        score(0, k)
        turn(k)
    for m in range(TEAM):
        top = jnp.max(peaks[m], axis=0, keepdims=True)
        if m + 1 < TEAM:
            begin(m + 1)
        for k in range(GROUP):
            raise_up(m, k, top)
            if m + 1 < TEAM:
                score(m + 1, k)
        if m + 1 < TEAM:
            turn(m + GROUP)
        scale = 1.0 / jnp.sum(sums[m][0], axis=0, keepdims=True)
        delta = jnp.sum(sums[m][1], axis=0, keepdims=True) * scale
        for k in range(GROUP):
            settle(m, k, scale, delta)
            if m and k == 1:
                query_side(m - 1)
            if m and k == 4:
                key_side(m - 1)
    query_side(TEAM - 1)
    for w in range(TEAM - 1, HALO + TEAM):
        key_side(w)


def attention(kind, *operands):
    def kernel(*refs):
        attention_kernel(kind, *refs)

    return pl.pallas_call(
        kernel,
        out_shape=(
            block_shape(TEAM),
            block_shape(TEAM, dtype=jnp.float32),
            block_shape(HALO),
        ),
        in_specs=smem() + vmem(len(operands) - 1),
        out_specs=tuple(vmem(3)),
        scratch_shapes=[
            pltpu.VMEM((PAIR, SPAN), jnp.bfloat16),
            pltpu.VMEM((2, GROUP, ROWS, BOTH), jnp.float32),
            pltpu.VMEM((SPAN, TEAM * BOTH), jnp.bfloat16),
            pltpu.VMEM((TEAM * BOTH, PAIR), jnp.bfloat16),
        ],
        compiler_params=pltpu.CompilerParams(vmem_limit_bytes=VMEM_BYTES),
        cost_estimate=pl.CostEstimate(flops=0, bytes_accessed=0, transcendentals=0),
        name="attention_cross" if kind == CROSS else "attention_self",
    )(*operands)


def join_kernel(own_s, own_c, home_s, home_c, out_c, out):
    for kind, own, home in ((SELF, own_s, home_s), (CROSS, own_c, home_c)):
        out[0, kind] = own[0].astype(jnp.bfloat16)
        for b in range(HALO):
            out[b + 1, kind] = (own[b + 1] + home[b].astype(jnp.float32)).astype(jnp.bfloat16)
    for b in range(TEAM):
        out[b, NEAR] = out_c[b]


def halves(first, second):
    left = jnp.concatenate([first[:, :HEAD], second[:, :HEAD]], axis=1)
    right = jnp.concatenate([first[:, HEAD:], second[:, HEAD:]], axis=1)
    return left, right


def unpack_kernel(parts, parts_s, attended, query_s, key_s, value_s, query_c, key_c, value_c):
    flip = my_flip()
    for h in range(0, HEADS, 2):
        lanes = pl.ds(h * HEAD, PAIR)
        left, right = jnp.bitwise_xor(h, flip), jnp.bitwise_xor(h + 1, flip)
        first, second = parts.at[left], parts.at[right]
        key_s[:, lanes], value_s[:, lanes] = halves(first[SELF], second[SELF])
        key_c[:, lanes], value_c[:, lanes] = halves(first[CROSS], second[CROSS])
        query_s[:, lanes], near = halves(parts_s[left], parts_s[right])
        query_c[:, lanes], far = halves(first[NEAR], second[NEAR])
        total = near.astype(jnp.float32) + far.astype(jnp.float32)
        attended[:, lanes] = total.astype(jnp.bfloat16)


def local_call(kernel, out_shape, in_specs, operands, name, scratch=()):
    return pl.pallas_call(
        kernel,
        out_shape=out_shape,
        in_specs=in_specs,
        out_specs=jax.tree.map(lambda shape: vmem(1)[0], out_shape),
        scratch_shapes=scratch,
        compiler_params=pltpu.CompilerParams(vmem_limit_bytes=VMEM_BYTES),
        cost_estimate=pl.CostEstimate(flops=0, bytes_accessed=0, transcendentals=0),
        name=name,
    )(*operands)


def to_next_team(value, step):
    count = lax.axis_size("ctx")
    route = [(i, (i + step * TEAM) % count ^ (TEAM // 2)) for i in range(count)]
    return lax.ppermute(value, "ctx", route)


def within_team(value):
    count = lax.axis_size("ctx")
    teams = [list(range(at, at + TEAM)) for at in range(0, count, TEAM)]
    return lax.all_to_all(value, "ctx", 0, 0, axis_index_groups=teams, tiled=True)


def swapped(value):
    return lax.ppermute(value, "tower", [(0, 1), (1, 0)])


def body(
    query_self, key_self, value_self, query_cross, key_cross, value_cross, cotangent, block_slot
):
    count = lax.axis_size("ctx")
    member = lax.rem(lax.axis_index("ctx"), TEAM)
    slots = jnp.stack([lax.rem(block_slot[0] - member + count, count), jnp.int32(count)])
    flat = jax.ShapeDtypeStruct((ROWS, FEATURES), jnp.bfloat16)
    inputs = (query_self, key_self, value_self, query_cross, key_cross, value_cross, cotangent)
    far, near = local_call(
        pack_kernel,
        (block_shape(TEAM), block_shape(TEAM, 3)),
        [pl.BlockSpec(memory_space=pltpu.HBM)] * 7,
        tuple(pltpu.with_memory_space_constraint(value[0], pltpu.HBM) for value in inputs),
        "pack",
        [pltpu.VMEM((7, ROWS, FEATURES), jnp.bfloat16), pltpu.SemaphoreType.DMA((7,))],
    )
    arrived = swapped(far)
    own = within_team(near)
    halo = to_next_team(own[1:, :NEAR], 1)
    crossing = within_team(arrived)
    out_s, own_s, back_s = attention(SELF, slots, own, halo)
    out_c, own_c, back_c = attention(CROSS, slots, crossing, own, halo)
    home_s = to_next_team(back_s, -1)
    home_c = to_next_team(back_c, -1)
    joined = local_call(
        join_kernel,
        block_shape(TEAM, 3),
        vmem(5),
        (own_s, own_c, home_s, home_c, swapped(out_c)),
        "join",
    )
    parts_s = within_team(out_s)
    outs = local_call(
        unpack_kernel, (flat,) * 7, vmem(2), (within_team(joined), parts_s), "unpack"
    )
    return tuple(part[None] for part in outs)


def solution(mesh):
    rows = P("tower", ("dp", "ctx"), None)
    return jax.shard_map(
        body,
        mesh=mesh,
        in_specs=(rows,) * 7 + (P("ctx"),),
        out_specs=(rows,) * 7,
        check_vma=False,
    )
```

```python
import jax
import jax.numpy as jnp
from jax import lax
from jax.experimental import pallas as pl
from jax.experimental.pallas import tpu as pltpu
from jax.sharding import PartitionSpec as P

HEADS = 8
HEAD = 64
ROWS = 128
GROUP = 8
TEAM = 8
PAIR = 2 * HEAD
BOTH = 2 * ROWS
HALO = GROUP - 1
WINDOW = GROUP * ROWS
SPAN = (HALO + TEAM) * ROWS
FEATURES = HEADS * HEAD
VMEM_BYTES = 48 * 1024 * 1024
SELF, CROSS, NEAR, FAR = 0, 1, 2, 3


def vmem(count):
    return [pl.BlockSpec(memory_space=pltpu.VMEM)] * count


def smem():
    return [pl.BlockSpec(memory_space=pltpu.SMEM)]


def block_shape(*lead, dtype=jnp.bfloat16):
    return jax.ShapeDtypeStruct((*lead, ROWS, PAIR), dtype)


def paired(left, right, h):
    lanes = pl.ds(h * HEAD, HEAD)
    return jnp.concatenate([left[:, lanes], right[:, lanes]], axis=1)


def my_flip():
    return lax.rem(lax.axis_index("ctx") // TEAM, 2) * (TEAM // 2)


def pack_kernel(
    query_s, key_s, value_s, query_c, key_c, value_c, upstream, far, near, held, arrived
):
    sources = (upstream, query_c, query_s, key_s, value_s, key_c, value_c)
    copies = [
        pltpu.make_async_copy(source, held.at[i], arrived.at[i])
        for i, source in enumerate(sources)
    ]
    for copy in copies:
        copy.start()
    flip = my_flip()
    copies[0].wait()
    for kind, left, right in ((FAR, 1, 0), (NEAR, 2, 0), (SELF, 3, 4), (CROSS, 5, 6)):
        copies[left].wait()
        if right:
            copies[right].wait()
        for h in range(HEADS):
            value = paired(held.at[left], held.at[right], h)
            if kind == FAR:
                far[jnp.bitwise_xor(h, flip)] = value
            else:
                near[jnp.bitwise_xor(h, flip), kind] = value


def attention_kernel(kind, slots, *refs):
    if kind == SELF:
        own, halo, out, dkv_own, dkv_halo, kv_t, scores, probs, stacks = refs
        queries = [own.at[b, NEAR] for b in range(TEAM)]
    else:
        qdo, own, halo, out, dkv_own, dkv_halo, kv_t, scores, probs, stacks = refs
        queries = [qdo.at[b] for b in range(TEAM)]
    blocks = [halo.at[b] for b in range(HALO)] + [own.at[b, kind] for b in range(TEAM)]
    first_half = lax.broadcasted_iota(jnp.int32, (ROWS, PAIR), 1) < HEAD
    causal = lax.broadcasted_iota(jnp.int32, (ROWS, ROWS), 0) <= lax.broadcasted_iota(
        jnp.int32, (ROWS, ROWS), 1
    )
    peaks, hidden, sums = {}, {}, {}

    def turn(w):
        kv_t[:, w * ROWS : (w + 1) * ROWS] = blocks[w][...].T

    def begin(m):
        both = queries[m][...]
        none = jnp.zeros_like(both)
        stacks[m * BOTH : m * BOTH + ROWS, :] = jnp.where(
            first_half, both * jnp.bfloat16(HEAD ** (-0.5)), none
        )
        stacks[m * BOTH + ROWS : (m + 1) * BOTH, :] = jnp.where(first_half, none, both)
        slot = lax.rem(slots[0] + m, slots[1])
        hidden[m] = [jnp.where(slot >= HALO - k, 0.0, 1e30) for k in range(HALO)] + [0.0]

    def score(m, k):
        part = lax.dot_general(
            blocks[m + k][...],
            stacks[m * BOTH : (m + 1) * BOTH, :],
            (((1,), (1,)), ((), ())),
            preferred_element_type=jnp.float32,
        )
        logits = part[:, :ROWS]
        if k == GROUP - 1:
            logits = jnp.where(causal, logits, -1e30)
        scores[m % 2, k, :, :ROWS] = logits
        scores[m % 2, k, :, ROWS:] = part[:, ROWS:]
        peak = jnp.max(logits.reshape(ROWS // 8, 8, ROWS), axis=0) - hidden[m][k]
        peaks[m] = peak if k == 0 else jnp.maximum(peaks[m], peak)

    def raise_up(m, k, top):
        raised = jnp.exp(scores[m % 2, k, :, :ROWS] - (top + hidden[m][k]))
        change = raised * scores[m % 2, k, :, ROWS:]
        scores[m % 2, k, :, :ROWS] = raised
        total = jnp.sum(raised.reshape(ROWS // 8, 8, ROWS), axis=0)
        weighted = jnp.sum(change.reshape(ROWS // 8, 8, ROWS), axis=0)
        sums[m] = (total, weighted) if k == 0 else (sums[m][0] + total, sums[m][1] + weighted)

    def settle(m, k, scale, delta):
        weight = scores[m % 2, k, :, :ROWS] * scale
        change = weight * (scores[m % 2, k, :, ROWS:] - delta)
        rows, lanes = slice((m + k) * ROWS, (m + k + 1) * ROWS), m * BOTH
        probs[rows, lanes : lanes + ROWS] = change.astype(jnp.bfloat16)
        probs[rows, lanes + ROWS : lanes + BOTH] = weight.astype(jnp.bfloat16)

    def query_side(m):
        window, lanes = slice(m * ROWS, m * ROWS + WINDOW), m * BOTH
        mixed = lax.dot_general(
            kv_t[:, window],
            probs[window, lanes : lanes + BOTH],
            (((1,), (0,)), ((), ())),
            preferred_element_type=jnp.float32,
        )
        result = jnp.concatenate(
            [mixed[:HEAD, :ROWS] * HEAD ** (-0.5), mixed[HEAD:, ROWS:]], axis=0
        )
        out[m] = result.T.astype(jnp.bfloat16)

    def key_side(w):
        low, high = max(0, w - HALO), min(TEAM - 1, w) + 1
        total = lax.dot_general(
            probs[w * ROWS : (w + 1) * ROWS, low * BOTH : high * BOTH],
            stacks[low * BOTH : high * BOTH, :],
            (((1,), (0,)), ((), ())),
            preferred_element_type=jnp.float32,
        )
        if w < HALO:
            dkv_halo[w] = total.astype(jnp.bfloat16)
        else:
            dkv_own[w - HALO] = total

    begin(0)
    for k in range(GROUP):
        score(0, k)
        turn(k)
    for m in range(TEAM):
        top = jnp.max(peaks[m], axis=0, keepdims=True)
        if m + 1 < TEAM:
            begin(m + 1)
        for k in range(GROUP):
            raise_up(m, k, top)
            if m + 1 < TEAM:
                score(m + 1, k)
        if m + 1 < TEAM:
            turn(m + GROUP)
        scale = 1.0 / jnp.sum(sums[m][0], axis=0, keepdims=True)
        delta = jnp.sum(sums[m][1], axis=0, keepdims=True) * scale
        for k in range(GROUP):
            settle(m, k, scale, delta)
            if m and k == 1:
                query_side(m - 1)
            if m and k == 4:
                key_side(m - 1)
    query_side(TEAM - 1)
    for w in range(TEAM - 1, HALO + TEAM):
        key_side(w)


def attention(kind, *operands):
    def kernel(*refs):
        attention_kernel(kind, *refs)

    return pl.pallas_call(
        kernel,
        out_shape=(
            block_shape(TEAM),
            block_shape(TEAM, dtype=jnp.float32),
            block_shape(HALO),
        ),
        in_specs=smem() + vmem(len(operands) - 1),
        out_specs=tuple(vmem(3)),
        scratch_shapes=[
            pltpu.VMEM((PAIR, SPAN), jnp.bfloat16),
            pltpu.VMEM((2, GROUP, ROWS, BOTH), jnp.float32),
            pltpu.VMEM((SPAN, TEAM * BOTH), jnp.bfloat16),
            pltpu.VMEM((TEAM * BOTH, PAIR), jnp.bfloat16),
        ],
        compiler_params=pltpu.CompilerParams(vmem_limit_bytes=VMEM_BYTES),
        cost_estimate=pl.CostEstimate(flops=0, bytes_accessed=0, transcendentals=0),
        name="attention_cross" if kind == CROSS else "attention_self",
    )(*operands)


def join_kernel(own_s, own_c, home_s, home_c, out_c, out):
    for kind, own, home in ((SELF, own_s, home_s), (CROSS, own_c, home_c)):
        out[0, kind] = own[0].astype(jnp.bfloat16)
        for b in range(HALO):
            out[b + 1, kind] = (own[b + 1] + home[b].astype(jnp.float32)).astype(jnp.bfloat16)
    for b in range(TEAM):
        out[b, NEAR] = out_c[b]


def halves(first, second):
    left = jnp.concatenate([first[:, :HEAD], second[:, :HEAD]], axis=1)
    right = jnp.concatenate([first[:, HEAD:], second[:, HEAD:]], axis=1)
    return left, right


def unpack_kernel(parts, parts_s, attended, query_s, key_s, value_s, query_c, key_c, value_c):
    flip = my_flip()
    for h in range(0, HEADS, 2):
        lanes = pl.ds(h * HEAD, PAIR)
        left, right = jnp.bitwise_xor(h, flip), jnp.bitwise_xor(h + 1, flip)
        first, second = parts.at[left], parts.at[right]
        key_s[:, lanes], value_s[:, lanes] = halves(first[SELF], second[SELF])
        key_c[:, lanes], value_c[:, lanes] = halves(first[CROSS], second[CROSS])
        query_s[:, lanes], near = halves(parts_s[left], parts_s[right])
        query_c[:, lanes], far = halves(first[NEAR], second[NEAR])
        total = near.astype(jnp.float32) + far.astype(jnp.float32)
        attended[:, lanes] = total.astype(jnp.bfloat16)


def local_call(kernel, out_shape, in_specs, operands, name, scratch=()):
    return pl.pallas_call(
        kernel,
        out_shape=out_shape,
        in_specs=in_specs,
        out_specs=jax.tree.map(lambda shape: vmem(1)[0], out_shape),
        scratch_shapes=scratch,
        compiler_params=pltpu.CompilerParams(vmem_limit_bytes=VMEM_BYTES),
        cost_estimate=pl.CostEstimate(flops=0, bytes_accessed=0, transcendentals=0),
        name=name,
    )(*operands)


def to_next_team(value, step):
    count = lax.axis_size("ctx")
    route = [(i, (i + step * TEAM) % count ^ (TEAM // 2)) for i in range(count)]
    return lax.ppermute(value, "ctx", route)


def within_team(value):
    count = lax.axis_size("ctx")
    teams = [list(range(at, at + TEAM)) for at in range(0, count, TEAM)]
    return lax.all_to_all(value, "ctx", 0, 0, axis_index_groups=teams, tiled=True)


def swapped(value):
    return lax.ppermute(value, "tower", [(0, 1), (1, 0)])


def body(
    query_self, key_self, value_self, query_cross, key_cross, value_cross, cotangent, block_slot
):
    count = lax.axis_size("ctx")
    member = lax.rem(lax.axis_index("ctx"), TEAM)
    slots = jnp.stack([lax.rem(block_slot[0] - member + count, count), jnp.int32(count)])
    flat = jax.ShapeDtypeStruct((ROWS, FEATURES), jnp.bfloat16)
    inputs = (query_self, key_self, value_self, query_cross, key_cross, value_cross, cotangent)
    far, near = local_call(
        pack_kernel,
        (block_shape(TEAM), block_shape(TEAM, 3)),
        [pl.BlockSpec(memory_space=pltpu.HBM)] * 7,
        tuple(pltpu.with_memory_space_constraint(value[0], pltpu.HBM) for value in inputs),
        "pack",
        [pltpu.VMEM((7, ROWS, FEATURES), jnp.bfloat16), pltpu.SemaphoreType.DMA((7,))],
    )
    arrived = swapped(far)
    own = within_team(near)
    halo_c = to_next_team(own[1:, CROSS], 1)
    halo_s = to_next_team(own[1:, SELF], 1)
    arrived, halo_c = lax.optimization_barrier((arrived, halo_c))
    crossing = within_team(arrived)
    out_s, own_s, back_s = attention(SELF, slots, own, halo_s)
    out_c, own_c, back_c = attention(CROSS, slots, crossing, own, halo_c)
    home_s = to_next_team(back_s, -1)
    home_c = to_next_team(back_c, -1)
    joined = local_call(
        join_kernel,
        block_shape(TEAM, 3),
        vmem(5),
        (own_s, own_c, home_s, home_c, swapped(out_c)),
        "join",
    )
    parts_s = within_team(out_s)
    outs = local_call(
        unpack_kernel, (flat,) * 7, vmem(2), (within_team(joined), parts_s), "unpack"
    )
    return tuple(part[None] for part in outs)


def solution(mesh):
    rows = P("tower", ("dp", "ctx"), None)
    return jax.shard_map(
        body,
        mesh=mesh,
        in_specs=(rows,) * 7 + (P("ctx"),),
        out_specs=(rows,) * 7,
        check_vma=False,
    )
```

```python
import jax
import jax.numpy as jnp
from jax import lax
from jax.experimental import pallas as pl
from jax.experimental.pallas import tpu as pltpu
from jax.sharding import PartitionSpec as P

HEADS = 8
HEAD = 64
ROWS = 128
GROUP = 8
TEAM = 8
PAIR = 2 * HEAD
BOTH = 2 * ROWS
HALO = GROUP - 1
WINDOW = GROUP * ROWS
SPAN = (HALO + TEAM) * ROWS
FEATURES = HEADS * HEAD
VMEM_BYTES = 48 * 1024 * 1024
SELF, CROSS, NEAR, FAR = 0, 1, 2, 3


def vmem(count):
    return [pl.BlockSpec(memory_space=pltpu.VMEM)] * count


def smem():
    return [pl.BlockSpec(memory_space=pltpu.SMEM)]


def block_shape(*lead, dtype=jnp.bfloat16):
    return jax.ShapeDtypeStruct((*lead, ROWS, PAIR), dtype)


def paired(left, right, h):
    lanes = pl.ds(h * HEAD, HEAD)
    return jnp.concatenate([left[:, lanes], right[:, lanes]], axis=1)


def my_flip():
    return lax.rem(lax.axis_index("ctx") // TEAM, 2) * (TEAM // 2)


def pack_kernel(
    query_s, key_s, value_s, query_c, key_c, value_c, upstream, far, near, held, arrived
):
    sources = (upstream, query_c, query_s, key_s, value_s, key_c, value_c)
    copies = [
        pltpu.make_async_copy(source, held.at[i], arrived.at[i])
        for i, source in enumerate(sources)
    ]
    for copy in copies:
        copy.start()
    flip = my_flip()
    copies[0].wait()
    for kind, left, right in ((FAR, 1, 0), (NEAR, 2, 0), (SELF, 3, 4), (CROSS, 5, 6)):
        copies[left].wait()
        if right:
            copies[right].wait()
        for h in range(HEADS):
            value = paired(held.at[left], held.at[right], h)
            if kind == FAR:
                far[jnp.bitwise_xor(h, flip)] = value
            else:
                near[jnp.bitwise_xor(h, flip), kind] = value


def attention_kernel(kind, slots, *refs):
    if kind == SELF:
        own, halo, out, dkv_own, dkv_halo, kv_t, scores, probs, stacks = refs
        queries = [own.at[b, NEAR] for b in range(TEAM)]
    else:
        qdo, own, halo, out, dkv_own, dkv_halo, kv_t, scores, probs, stacks = refs
        queries = [qdo.at[b] for b in range(TEAM)]
    blocks = [halo.at[b, kind] for b in range(HALO)] + [own.at[b, kind] for b in range(TEAM)]
    first_half = lax.broadcasted_iota(jnp.int32, (ROWS, PAIR), 1) < HEAD
    causal = lax.broadcasted_iota(jnp.int32, (ROWS, ROWS), 0) <= lax.broadcasted_iota(
        jnp.int32, (ROWS, ROWS), 1
    )
    peaks, hidden, sums = {}, {}, {}

    def turn(w):
        kv_t[:, w * ROWS : (w + 1) * ROWS] = blocks[w][...].T

    def begin(m):
        both = queries[m][...]
        none = jnp.zeros_like(both)
        stacks[m * BOTH : m * BOTH + ROWS, :] = jnp.where(
            first_half, both * jnp.bfloat16(HEAD ** (-0.5)), none
        )
        stacks[m * BOTH + ROWS : (m + 1) * BOTH, :] = jnp.where(first_half, none, both)
        slot = lax.rem(slots[0] + m, slots[1])
        hidden[m] = [jnp.where(slot >= HALO - k, 0.0, 1e30) for k in range(HALO)] + [0.0]

    def score(m, k):
        part = lax.dot_general(
            blocks[m + k][...],
            stacks[m * BOTH : (m + 1) * BOTH, :],
            (((1,), (1,)), ((), ())),
            preferred_element_type=jnp.float32,
        )
        logits = part[:, :ROWS]
        if k == GROUP - 1:
            logits = jnp.where(causal, logits, -1e30)
        scores[m % 2, k, :, :ROWS] = logits
        scores[m % 2, k, :, ROWS:] = part[:, ROWS:]
        peak = jnp.max(logits.reshape(ROWS // 8, 8, ROWS), axis=0) - hidden[m][k]
        peaks[m] = peak if k == 0 else jnp.maximum(peaks[m], peak)

    def raise_up(m, k, top):
        raised = jnp.exp(scores[m % 2, k, :, :ROWS] - (top + hidden[m][k]))
        change = raised * scores[m % 2, k, :, ROWS:]
        scores[m % 2, k, :, :ROWS] = raised
        total = jnp.sum(raised.reshape(ROWS // 8, 8, ROWS), axis=0)
        weighted = jnp.sum(change.reshape(ROWS // 8, 8, ROWS), axis=0)
        sums[m] = (total, weighted) if k == 0 else (sums[m][0] + total, sums[m][1] + weighted)

    def settle(m, k, scale, delta):
        weight = scores[m % 2, k, :, :ROWS] * scale
        change = weight * (scores[m % 2, k, :, ROWS:] - delta)
        rows, lanes = slice((m + k) * ROWS, (m + k + 1) * ROWS), m * BOTH
        probs[rows, lanes : lanes + ROWS] = change.astype(jnp.bfloat16)
        probs[rows, lanes + ROWS : lanes + BOTH] = weight.astype(jnp.bfloat16)

    def query_side(m):
        window, lanes = slice(m * ROWS, m * ROWS + WINDOW), m * BOTH
        mixed = lax.dot_general(
            kv_t[:, window],
            probs[window, lanes : lanes + BOTH],
            (((1,), (0,)), ((), ())),
            preferred_element_type=jnp.float32,
        )
        result = jnp.concatenate(
            [mixed[:HEAD, :ROWS] * HEAD ** (-0.5), mixed[HEAD:, ROWS:]], axis=0
        )
        out[m] = result.T.astype(jnp.bfloat16)

    def key_terms(w, low, high):
        return lax.dot_general(
            probs[w * ROWS : (w + 1) * ROWS, low * BOTH : high * BOTH],
            stacks[low * BOTH : high * BOTH, :],
            (((1,), (0,)), ((), ())),
            preferred_element_type=jnp.float32,
        )

    def key_side(w):
        total = key_terms(w, max(0, w - HALO), min(TEAM - 1, w) + 1)
        if w < HALO:
            dkv_halo[w] = total.astype(jnp.bfloat16)
        else:
            dkv_own[w - HALO] = total

    begin(0)
    for k in range(GROUP):
        score(0, k)
        turn(k)
    for m in range(TEAM):
        top = jnp.max(peaks[m], axis=0, keepdims=True)
        if m + 1 < TEAM:
            begin(m + 1)
        for k in range(GROUP):
            raise_up(m, k, top)
            if m + 1 < TEAM:
                score(m + 1, k)
            elif k < HALO - 1:
                dkv_own[k + 1] = key_terms(TEAM + k, k + 1, TEAM - 1)
        if m + 1 < TEAM:
            turn(m + GROUP)
        scale = 1.0 / jnp.sum(sums[m][0], axis=0, keepdims=True)
        delta = jnp.sum(sums[m][1], axis=0, keepdims=True) * scale
        for k in range(GROUP):
            settle(m, k, scale, delta)
            if m and k == 1:
                query_side(m - 1)
            if m and k == 4:
                key_side(m - 1)
    query_side(TEAM - 1)
    key_side(TEAM - 1)
    for b in range(1, TEAM - 1):
        dkv_own[b] += key_terms(b + HALO, TEAM - 1, TEAM)
    key_side(HALO + TEAM - 1)


def attention(kind, *operands):
    def kernel(*refs):
        attention_kernel(kind, *refs)

    return pl.pallas_call(
        kernel,
        out_shape=(
            block_shape(TEAM),
            block_shape(TEAM, dtype=jnp.float32),
            block_shape(HALO),
        ),
        in_specs=smem() + vmem(len(operands) - 1),
        out_specs=tuple(vmem(3)),
        scratch_shapes=[
            pltpu.VMEM((PAIR, SPAN), jnp.bfloat16),
            pltpu.VMEM((2, GROUP, ROWS, BOTH), jnp.float32),
            pltpu.VMEM((SPAN, TEAM * BOTH), jnp.bfloat16),
            pltpu.VMEM((TEAM * BOTH, PAIR), jnp.bfloat16),
        ],
        compiler_params=pltpu.CompilerParams(vmem_limit_bytes=VMEM_BYTES),
        cost_estimate=pl.CostEstimate(flops=0, bytes_accessed=0, transcendentals=0),
        name="attention_cross" if kind == CROSS else "attention_self",
    )(*operands)


def join_kernel(own_s, own_c, home_s, home_c, out_c, out):
    for kind, own, home in ((SELF, own_s, home_s), (CROSS, own_c, home_c)):
        out[0, kind] = own[0].astype(jnp.bfloat16)
        for b in range(HALO):
            out[b + 1, kind] = (own[b + 1] + home[b].astype(jnp.float32)).astype(jnp.bfloat16)
    for b in range(TEAM):
        out[b, NEAR] = out_c[b]


def halves(first, second):
    left = jnp.concatenate([first[:, :HEAD], second[:, :HEAD]], axis=1)
    right = jnp.concatenate([first[:, HEAD:], second[:, HEAD:]], axis=1)
    return left, right


def unpack_kernel(parts, parts_s, attended, query_s, key_s, value_s, query_c, key_c, value_c):
    flip = my_flip()
    for h in range(0, HEADS, 2):
        lanes = pl.ds(h * HEAD, PAIR)
        left, right = jnp.bitwise_xor(h, flip), jnp.bitwise_xor(h + 1, flip)
        first, second = parts.at[left], parts.at[right]
        key_s[:, lanes], value_s[:, lanes] = halves(first[SELF], second[SELF])
        key_c[:, lanes], value_c[:, lanes] = halves(first[CROSS], second[CROSS])
        query_s[:, lanes], near = halves(parts_s[left], parts_s[right])
        query_c[:, lanes], far = halves(first[NEAR], second[NEAR])
        total = near.astype(jnp.float32) + far.astype(jnp.float32)
        attended[:, lanes] = total.astype(jnp.bfloat16)


def local_call(kernel, out_shape, in_specs, operands, name, scratch=()):
    return pl.pallas_call(
        kernel,
        out_shape=out_shape,
        in_specs=in_specs,
        out_specs=jax.tree.map(lambda shape: vmem(1)[0], out_shape),
        scratch_shapes=scratch,
        compiler_params=pltpu.CompilerParams(vmem_limit_bytes=VMEM_BYTES),
        cost_estimate=pl.CostEstimate(flops=0, bytes_accessed=0, transcendentals=0),
        name=name,
    )(*operands)


def to_next_team(value, step):
    count = lax.axis_size("ctx")
    route = [(i, (i + step * TEAM) % count ^ (TEAM // 2)) for i in range(count)]
    return lax.ppermute(value, "ctx", route)


def within_team(value):
    count = lax.axis_size("ctx")
    teams = [list(range(at, at + TEAM)) for at in range(0, count, TEAM)]
    return lax.all_to_all(value, "ctx", 0, 0, axis_index_groups=teams, tiled=True)


def swapped(value):
    return lax.ppermute(value, "tower", [(0, 1), (1, 0)])


def body(
    query_self, key_self, value_self, query_cross, key_cross, value_cross, cotangent, block_slot
):
    count = lax.axis_size("ctx")
    member = lax.rem(lax.axis_index("ctx"), TEAM)
    slots = jnp.stack([lax.rem(block_slot[0] - member + count, count), jnp.int32(count)])
    flat = jax.ShapeDtypeStruct((ROWS, FEATURES), jnp.bfloat16)
    inputs = (query_self, key_self, value_self, query_cross, key_cross, value_cross, cotangent)
    far, near = local_call(
        pack_kernel,
        (block_shape(TEAM), block_shape(TEAM, 3)),
        [pl.BlockSpec(memory_space=pltpu.HBM)] * 7,
        tuple(pltpu.with_memory_space_constraint(value[0], pltpu.HBM) for value in inputs),
        "pack",
        [pltpu.VMEM((7, ROWS, FEATURES), jnp.bfloat16), pltpu.SemaphoreType.DMA((7,))],
    )
    arrived = swapped(far)
    own = within_team(near)
    halo = to_next_team(own[1:, :NEAR], 1)
    crossing = within_team(arrived)
    out_s, own_s, back_s = attention(SELF, slots, own, halo)
    out_c, own_c, back_c = attention(CROSS, slots, crossing, own, halo)
    home_s = to_next_team(back_s, -1)
    home_c = to_next_team(back_c, -1)
    joined = local_call(
        join_kernel,
        block_shape(TEAM, 3),
        vmem(5),
        (own_s, own_c, home_s, home_c, swapped(out_c)),
        "join",
    )
    parts_s = within_team(out_s)
    outs = local_call(
        unpack_kernel, (flat,) * 7, vmem(2), (within_team(joined), parts_s), "unpack"
    )
    return tuple(part[None] for part in outs)


def solution(mesh):
    rows = P("tower", ("dp", "ctx"), None)
    return jax.shard_map(
        body,
        mesh=mesh,
        in_specs=(rows,) * 7 + (P("ctx"),),
        out_specs=(rows,) * 7,
        check_vma=False,
    )
```
